512 devices in a mesh: dp: 16 (over z_lo, core), tm: 32 (over y, z_hi, x).
Axes of the slice: x: 4, y: 4, z: 16 (z_hi: 2, z_lo: 8; z = z_hi * 8 + z_lo), core: 2. Of those that a mesh axis runs over, the one named last changes fastest.
Arguments:
- query_rows: bfloat16 [16, 4096, 1024], P('dp', 'tm'), may hold values from -24 to 24
- key_rows: bfloat16 [16, 4096, 1024], P('dp', 'tm'), may hold values from -24 to 24
- value_rows: bfloat16 [16, 4096, 1024], P('dp', 'tm'), may hold values from -6 to 6
- grad_out: bfloat16 [16, 4096, 1024], P('dp', 'tm'), may hold values from -6 to 6
- conv_weight: float32 [9, 1024], replicated, may hold values from -0.6 to 0.6
- frames: int32 [16], P('dp'), may hold values from 2048 to 4096, as said below
- window_links: int32 [16, 32, 2], P('dp', 'tm'), may hold values 0 or 1
Outputs:
- grad_query: bfloat16 [16, 4096, 1024], P('dp', 'tm')
- grad_key: bfloat16 [16, 4096, 1024], P('dp', 'tm')
- grad_value: bfloat16 [16, 4096, 1024], P('dp', 'tm')
- grad_conv: float32 [9, 1024], replicated
The draws below stay inside these ranges and needn't reach their ends.
Inputs may be any that keep to these rules, and one draw needn't show every extreme that they name: Some recording has all 4096 frames valid.
All inputs are finite; a program needn't handle non-finite values. No bound on the sum of `window_links` on one device may be relied on, other than what follows from the above.
Results may differ from the reference program's by a relative error of at most 0.015.
Values may be sent and summed in bfloat16 or wider, within the bound.
No kernel may reach another device: no remote copies, remote signals or barrier semaphores. Data moves between devices by JAX's collectives and lax.ppermute only.
A program may use at most 64 MiB of HBM per device.

```python
import jax
import jax.numpy as jnp
from jax import lax

D = 1024
H = 8
KW = 9
BLK = 128
HALF = 4
SEQ = 4096
NBLK = 32
G = 256
POOL = 16
N_DP = 16


def draw_query_rows(key, part):
    result = jnp.clip(jax.random.normal(jax.random.fold_in(key, 303), (N_DP, SEQ, D), jnp.float32), -4.0, 4.0)
    return result.astype(jnp.bfloat16)


def draw_key_rows(key, part):
    result = jnp.clip(jax.random.normal(jax.random.fold_in(key, 505), (N_DP, SEQ, D), jnp.float32), -4.0, 4.0)
    return result.astype(jnp.bfloat16)


def draw_frames(key, part):
    counts = jax.random.randint(jax.random.fold_in(key, 606), (N_DP,), SEQ // 2, SEQ + 1)
    chosen = jax.random.randint(jax.random.fold_in(key, 707), (), 0, N_DP)
    return jnp.where(jnp.arange(N_DP) == chosen, SEQ, counts).astype(jnp.int32)


def plant(drawn, stream_key, low, high):
    spot = [jax.random.randint(jax.random.fold_in(stream_key, axis), (), 0, length) for axis, length in enumerate(drawn.shape)]
    widest = drawn.shape.index(max(drawn.shape))
    next_to = spot[:widest] + [(spot[widest] + 1) % drawn.shape[widest]] + spot[widest + 1:]
    return drawn.at[tuple(spot)].set(low).at[tuple(next_to)].set(high)


def shard_levels(own_key, dims, pieces, least, largest):
    factor_of = 1.0
    for dim, shards_of in pieces:
        steps = jax.random.uniform(jax.random.fold_in(jax.random.fold_in(own_key, 6), dim), (shards_of,), jnp.float32, least / len(pieces), largest / len(pieces))
        factor_of = factor_of * jnp.repeat(jnp.exp(steps), dims[dim] // shards_of).reshape((-1,) + (1,) * (len(dims) - 1 - dim))
    return factor_of


def gaussian(own_key, shape, width, most, cuts=(), kind=jnp.bfloat16):
    array = jax.random.normal(own_key, shape, jnp.float32) * width
    if len(cuts) > 0:
        array = shard_levels(own_key, shape, cuts, -0.22, 0.18) * array
    return jnp.clip(array, min=-most, max=most).astype(kind)


def setup_inputs(seed: int = 0) -> dict:
    keys = jax.random.split(jax.random.key(seed), 8)
    query_rows = draw_query_rows(jax.random.fold_in(keys[7], 71), 0)
    key_rows = draw_key_rows(jax.random.fold_in(keys[7], 71), 0)
    value_rows = gaussian(keys[2], (N_DP, SEQ, D), 1.0, 6.0, ((0, 16), (1, 32)))
    grad_out = gaussian(keys[3], (N_DP, SEQ, D), 1.0, 6.0, ((0, 16), (1, 32)))
    conv_weight = jnp.clip(jax.random.uniform(keys[4], (KW, D), jnp.float32, -0.6, 0.6), -0.6, 0.6)
    frames = draw_frames(jax.random.fold_in(keys[7], 71), 0)
    window_links = plant((jax.random.randint(keys[6], (N_DP, NBLK, 2), 0, 4) < 3).astype(jnp.int32), jax.random.fold_in(keys[6], 1), 0, 1)
    return {"query_rows": query_rows, "key_rows": key_rows, "value_rows": value_rows, "grad_out": grad_out, "conv_weight": conv_weight, "frames": frames, "window_links": window_links}


MASKED = -1e+30

def product(form, left_op, right_op):
    return jnp.einsum(form, left_op.astype(jnp.float32), right_op.astype(jnp.float32))

def unwind_window(window, blocks, block_rows, group_cols):
    parts = window.reshape(blocks, 3, block_rows, group_cols)
    spread = jnp.pad(parts[:, 0], ((0, 2), (0, 0), (0, 0)))
    spread = spread + jnp.pad(parts[:, 1], ((1, 1), (0, 0), (0, 0)))
    spread = spread + jnp.pad(parts[:, 2], ((2, 0), (0, 0), (0, 0)))
    return spread.reshape((blocks + 2) * block_rows, group_cols)

def block_pass(queries, padded_kv, pad_ok, link_rows, summary, summary_ok, attn_grad, block_rows, heads):
    row_count, full_width = queries.shape
    blocks = row_count // block_rows
    head_size = full_width // heads
    per_group = min(4, heads)
    group_cols = per_group * head_size
    glob_rows = summary.shape[0]
    score_scale = head_size ** (-0.5)
    ok_blocks = pad_ok.reshape(blocks + 2, block_rows)
    left_link = link_rows[:, 0:1] == 1
    right_link = link_rows[:, 1:2] == 1
    window_ok = jnp.concatenate([ok_blocks[:-2] & left_link, ok_blocks[1:-1], ok_blocks[2:] & right_link], axis=1)
    anchor = jnp.zeros((), jnp.int32)

    def one_group(group_index, running):
        attn_all, query_all, kv_all, summary_all = running
        column = (group_index * group_cols).astype(jnp.int32)
        other = (column + full_width).astype(jnp.int32)
        query_part = lax.dynamic_slice_in_dim(queries, column, group_cols, 1).reshape(blocks, block_rows, per_group, head_size)
        key_pad = lax.dynamic_slice_in_dim(padded_kv, column, group_cols, 1).reshape(blocks + 2, block_rows, per_group, head_size)
        value_pad = lax.dynamic_slice_in_dim(padded_kv, other, group_cols, 1).reshape(blocks + 2, block_rows, per_group, head_size)
        key_window = jnp.concatenate([key_pad[:-2], key_pad[1:-1], key_pad[2:]], axis=1)
        value_window = jnp.concatenate([value_pad[:-2], value_pad[1:-1], value_pad[2:]], axis=1)
        key_summary = lax.dynamic_slice_in_dim(summary, column, group_cols, 1).reshape(glob_rows, per_group, head_size)
        value_summary = lax.dynamic_slice_in_dim(summary, other, group_cols, 1).reshape(glob_rows, per_group, head_size)
        grad_part = lax.dynamic_slice_in_dim(attn_grad, column, group_cols, 1).reshape(blocks, block_rows, per_group, head_size)
        local_scores = product('cihd,cjhd->chij', query_part, key_window) * score_scale
        global_scores = product('cihd,ghd->chig', query_part, key_summary) * score_scale
        local_scores = jnp.where(window_ok[:, None, None, :], local_scores, MASKED)
        global_scores = jnp.where(summary_ok[None, None, None, :], global_scores, MASKED)
        highest = jnp.maximum(lax.optimization_barrier(jnp.max(local_scores, axis=-1)), lax.optimization_barrier(jnp.max(global_scores, axis=-1)))[..., None]
        local_exp = jnp.exp(local_scores - highest)
        global_exp = jnp.exp(global_scores - highest)
        row_total = lax.optimization_barrier(jnp.sum(local_exp, axis=-1, keepdims=True)) + lax.optimization_barrier(jnp.sum(global_exp, axis=-1, keepdims=True))
        local_prob = local_exp / row_total
        global_prob = global_exp / row_total
        local_pbf = local_prob.astype(jnp.bfloat16)
        global_pbf = global_prob.astype(jnp.bfloat16)
        mixed = product('chij,cjhd->cihd', local_pbf, value_window) + product('chig,ghd->cihd', global_pbf, value_summary)
        attn_part = mixed.astype(jnp.bfloat16)
        delta = product('cihd,cihd->chi', grad_part, attn_part)[..., None]
        local_dprob = product('cihd,cjhd->chij', grad_part, value_window)
        global_dprob = product('cihd,ghd->chig', grad_part, value_summary)
        local_dscore = (local_prob * (local_dprob - delta)).astype(jnp.bfloat16)
        global_dscore = (global_prob * (global_dprob - delta)).astype(jnp.bfloat16)
        query_grad = (product('chij,cjhd->cihd', local_dscore, key_window) + product('chig,ghd->cihd', global_dscore, key_summary)) * score_scale
        key_wgrad = product('chij,cihd->cjhd', local_dscore, query_part) * score_scale
        value_wgrad = product('chij,cihd->cjhd', local_pbf, grad_part)
        key_sgrad = product('chig,cihd->ghd', global_dscore, query_part) * score_scale
        value_sgrad = product('chig,cihd->ghd', global_pbf, grad_part)
        attn_all = lax.dynamic_update_slice(attn_all, attn_part.reshape(row_count, group_cols), (anchor, column))
        query_all = lax.dynamic_update_slice(query_all, query_grad.reshape(row_count, group_cols), (anchor, column))
        kv_all = lax.dynamic_update_slice(kv_all, unwind_window(key_wgrad, blocks, block_rows, group_cols), (anchor, column))
        kv_all = lax.dynamic_update_slice(kv_all, unwind_window(value_wgrad, blocks, block_rows, group_cols), (anchor, other))
        summary_all = lax.dynamic_update_slice(summary_all, key_sgrad.reshape(glob_rows, group_cols), (anchor, column))
        summary_all = lax.dynamic_update_slice(summary_all, value_sgrad.reshape(glob_rows, group_cols), (anchor, other))
        return (attn_all, query_all, kv_all, summary_all)
    start_state = (jnp.zeros((row_count, full_width), jnp.bfloat16), jnp.zeros((row_count, full_width), jnp.float32), jnp.zeros((row_count + 2 * block_rows, 2 * full_width), jnp.float32), jnp.zeros((glob_rows, 2 * full_width), jnp.float32))
    return lax.fori_loop(0, heads // per_group, one_group, start_state)

def conv_input_grad(grad_pad, conv_weight, row_count, half_width):
    accum = grad_pad[half_width:half_width + row_count].astype(jnp.float32)
    for shift_index in range(conv_weight.shape[0]):
        start = 2 * half_width - shift_index
        accum = accum + conv_weight[shift_index] * grad_pad[start:start + row_count].astype(jnp.float32)
    return accum.astype(jnp.bfloat16)

def conv_weight_grad(left_rows, right_pad, row_count, kernel):
    terms = []
    for shift_index in range(kernel):
        terms.append(lax.optimization_barrier(jnp.sum(left_rows.astype(jnp.float32) * right_pad[shift_index:shift_index + row_count].astype(jnp.float32), axis=0)))
    return jnp.stack(terms)

def pool_weights(valid_rows, pools):
    pool_valid = valid_rows.reshape(pools, -1).astype(jnp.float32)
    counts = lax.optimization_barrier(jnp.sum(pool_valid, axis=1, keepdims=True))
    return (pool_valid / jnp.maximum(counts, 1.0)).reshape(-1)

def pooled(key_value, share, pools):
    weighted = key_value.astype(jnp.float32).reshape(pools, -1, key_value.shape[1]) * share.reshape(pools, -1, 1)
    return lax.optimization_barrier(jnp.sum(weighted, axis=1)).astype(jnp.bfloat16)

def reference(query_rows, key_rows, value_rows, grad_out, conv_weight, frames, window_links):

    def one_recording(operands):
        queries, keys_here, values_here, grad_here, frame_count, link_rows = operands
        seq_rows = queries.shape[0]
        position = jnp.arange(seq_rows, dtype=jnp.int32)
        valid_rows = position < frame_count
        masked_grad = jnp.where(valid_rows[:, None], grad_here, jnp.zeros_like(grad_here))
        grad_pad = jnp.pad(masked_grad, ((HALF, HALF), (0, 0)))
        attn_grad = conv_input_grad(grad_pad, conv_weight, seq_rows, HALF)
        key_value = jnp.concatenate([keys_here, values_here], axis=1)
        share = pool_weights(valid_rows, G)
        summary = pooled(key_value, share, G)
        summary_ok = jnp.arange(G, dtype=jnp.int32) * POOL < frame_count
        padded_kv = jnp.pad(key_value, ((BLK, BLK), (0, 0)))
        pad_pos = jnp.arange(seq_rows + 2 * BLK, dtype=jnp.int32) - BLK
        pad_ok = (pad_pos >= 0) & (pad_pos < frame_count)
        attn_out, query_grad, kv_grad_pad, summary_grad = block_pass(queries, padded_kv, pad_ok, link_rows, summary, summary_ok, attn_grad, BLK, H)
        attn_pad = jnp.pad(attn_out, ((HALF, HALF), (0, 0)))
        kernel_grad = conv_weight_grad(masked_grad, attn_pad, seq_rows, KW)
        kv_grad = kv_grad_pad[BLK:BLK + seq_rows] + jnp.repeat(summary_grad, POOL, axis=0) * share[:, None]
        width_all = queries.shape[1]
        return (query_grad.astype(jnp.bfloat16), kv_grad[:, :width_all].astype(jnp.bfloat16), kv_grad[:, width_all:].astype(jnp.bfloat16), kernel_grad)
    grad_query, grad_key, grad_value, kernel_parts = lax.map(one_recording, (query_rows, key_rows, value_rows, grad_out, frames, window_links))
    return (grad_query, grad_key, grad_value, lax.optimization_barrier(jnp.sum(kernel_parts, axis=0)))
```

```python
import functools

import jax
import jax.numpy as jnp
from jax import lax
from jax.experimental import pallas as pl
from jax.experimental.pallas import tpu as pltpu
from jax.sharding import Mesh
from jax.sharding import PartitionSpec as P

H = 8
HD = 128
BLK = 128
POOL = 16
SUMM = BLK // POOL
KW = 9
HALF = 4
WIN = 3 * BLK
ROWS = WIN + 256
SCALE = HD ** (-0.5)
MASKED = -1e30
AXES = (("zl", 8), ("core", 2), ("y", 4), ("zh", 2), ("x", 4))
DP = ("zl", "core")
TM = ("y", "zh", "x")
PLANE = ("y", "x")
LINE = ("zl", "core", "zh")


def pack_kernel(info, k_ref, v_ref, go_ref, packed_ref, summary_ref):
    first, frame_count = info[0], info[1]
    row = first + lax.broadcasted_iota(jnp.int32, (BLK, 1), 0)
    grad = go_ref[...].astype(jnp.float32)
    grad = jnp.where(row < frame_count, grad, 0.0).astype(jnp.bfloat16)
    packed_ref[0, :BLK, :] = k_ref[...]
    packed_ref[1, :BLK, :] = v_ref[...]
    packed_ref[0, BLK:, :] = grad[BLK - 8 :]
    packed_ref[1, BLK:, :] = grad[:8]
    pool = lax.broadcasted_iota(jnp.int32, (SUMM, 1, 1), 0) * POOL + first
    count = jnp.clip(frame_count - pool, 0, POOL)
    frame = pool + lax.broadcasted_iota(jnp.int32, (SUMM, POOL, 1), 1)
    share = jnp.where(
        frame < frame_count, 1.0 / jnp.maximum(count, 1).astype(jnp.float32), 0.0
    )
    for side, ref in ((0, k_ref), (1, v_ref)):
        rows = ref[...].astype(jnp.float32).reshape(SUMM, POOL, ref.shape[1])
        summary_ref[side] = jnp.sum(rows * share, axis=1).astype(jnp.bfloat16)


def pack(info, keys, values, grad_out):
    width = keys.shape[1]
    whole = pl.BlockSpec(memory_space=pltpu.VMEM)
    return pl.pallas_call(
        pack_kernel,
        out_shape=(
            jax.ShapeDtypeStruct((2, BLK + 8, width), jnp.bfloat16),
            jax.ShapeDtypeStruct((2, SUMM, width), jnp.bfloat16),
        ),
        in_specs=[pl.BlockSpec(memory_space=pltpu.SMEM), whole, whole, whole],
        out_specs=(whole, whole),
        compiler_params=pltpu.CompilerParams(vmem_limit_bytes=32 * 2**20),
        name="pack",
    )(info, keys, values, grad_out)


def dot(left, right, contract):
    return lax.dot_general(
        left, right, (contract, ((), ())), preferred_element_type=jnp.float32
    )


NN = ((1,), (0,))
NT = ((1,), (1,))
TN = ((0,), (0,))


def attend_kernel(
    info,
    q_ref,
    k_ref,
    v_ref,
    go_ref,
    prev_ref,
    next_ref,
    prev_go_ref,
    next_go_ref,
    summary_ref,
    w_ref,
    dq_ref,
    center_ref,
    to_prev_ref,
    to_next_ref,
    dsum_ref,
    conv_ref,
    bias_ref,
):
    first, frame_count, left, right, z_half = (info[i] for i in range(5))

    @pl.when(pl.program_id(0) == 0)
    def _():
        row = lax.broadcasted_iota(jnp.int32, (BLK, HD), 0)
        seen_left = jnp.where(left == 1, frame_count - first + BLK, 0)
        seen_right = jnp.where(right == 1, frame_count - first - BLK, 0)
        for part, seen in enumerate((seen_left, frame_count - first, seen_right)):
            bias_ref[pl.ds(part * BLK, BLK), :] = jnp.where(row < seen, 0.0, MASKED)
        row = lax.broadcasted_iota(jnp.int32, (ROWS - WIN, HD), 0)
        source, half, pool = row >> 4, (row >> 3) & 1, row & 7
        block = ((source >> 2) * 2 + (half ^ z_half)) * 4 + (source & 3)
        start = (block * SUMM + pool) * POOL
        bias_ref[WIN:, :] = jnp.where(start < frame_count, 0.0, MASKED)

    summary = summary_ref[...]
    keys = jnp.concatenate(
        [prev_ref[0], k_ref[...], next_ref[0], summary[:, 0].reshape(-1, HD)], axis=0
    )
    values = jnp.concatenate(
        [prev_ref[1], v_ref[...], next_ref[1], summary[:, 1].reshape(-1, HD)], axis=0
    )
    queries = q_ref[...]

    row = first + lax.broadcasted_iota(jnp.int32, (BLK, 1), 0)
    grad = jnp.where(row < frame_count, go_ref[...].astype(jnp.float32), 0.0)
    reach = jnp.concatenate(
        [prev_go_ref[0].astype(jnp.float32), grad, next_go_ref[0].astype(jnp.float32)],
        axis=0,
    )
    shifted = [reach[8 + HALF - j : 8 + HALF - j + BLK] for j in range(KW)]
    total = grad
    for j in range(KW):
        total = total + w_ref[j : j + 1, :] * shifted[j]
    grad_attn = total.astype(jnp.bfloat16)

    scores = dot(keys, queries, NT) * SCALE + bias_ref[...]
    top = jnp.max(scores, axis=0, keepdims=True)
    weight = jnp.exp(scores - top)
    prob = weight * (1.0 / jnp.sum(weight, axis=0, keepdims=True))
    prob_bf = prob.astype(jnp.bfloat16)
    attn = dot(prob_bf, values, TN).astype(jnp.bfloat16).astype(jnp.float32)
    delta = jnp.sum(
        (grad_attn.astype(jnp.float32) * attn).T, axis=0, keepdims=True
    )
    dprob = dot(values, grad_attn, NT)
    dscore = (prob * (dprob - delta)).astype(jnp.bfloat16)

    dq_ref[...] = (dot(dscore, keys, TN) * SCALE).astype(jnp.bfloat16)
    for side, part in (
        (0, dot(dscore, queries, NN) * SCALE),
        (1, dot(prob_bf, grad_attn, NN)),
    ):
        to_prev_ref[side] = part[:BLK].astype(jnp.bfloat16)
        center_ref[side] = part[BLK : 2 * BLK]
        to_next_ref[side] = part[2 * BLK : WIN].astype(jnp.bfloat16)
        dsum_ref[:, side] = (
            part[WIN:].astype(jnp.bfloat16).reshape(dsum_ref.shape[0], 2 * SUMM, HD)
        )
    conv_ref[...] = jnp.concatenate(
        [jnp.sum(attn * shifted[j], axis=0, keepdims=True) for j in range(KW)]
        + [jnp.zeros((16 - KW, HD), jnp.float32)],
        axis=0,
    )


def attend(info, queries, keys, values, grad_out, prev, next_, summary, taps):
    width = queries.shape[1]
    own = pl.BlockSpec((BLK, HD), lambda h: (0, h))
    pair = pl.BlockSpec((2, BLK, HD), lambda h: (0, 0, h))
    many = pl.BlockSpec((16, 2, 2 * SUMM, HD), lambda h: (0, 0, 0, h))
    rim = BLK // 8
    return pl.pallas_call(
        attend_kernel,
        grid=(width // HD,),
        out_shape=(
            jax.ShapeDtypeStruct((BLK, width), jnp.bfloat16),
            jax.ShapeDtypeStruct((2, BLK, width), jnp.float32),
            jax.ShapeDtypeStruct((2, BLK, width), jnp.bfloat16),
            jax.ShapeDtypeStruct((2, BLK, width), jnp.bfloat16),
            jax.ShapeDtypeStruct((16, 2, 2 * SUMM, width), jnp.bfloat16),
            jax.ShapeDtypeStruct((16, width), jnp.float32),
        ),
        in_specs=[
            pl.BlockSpec(memory_space=pltpu.SMEM),
            own,
            own,
            own,
            own,
            pair,
            pair,
            pl.BlockSpec((1, 8, HD), lambda h: (0, rim, h)),
            pl.BlockSpec((1, 8, HD), lambda h: (1, rim, h)),
            many,
            pl.BlockSpec((KW, HD), lambda h: (0, h)),
        ],
        out_specs=(
            own,
            pair,
            pair,
            pair,
            many,
            pl.BlockSpec((16, HD), lambda h: (0, h)),
        ),
        scratch_shapes=[pltpu.VMEM((ROWS, HD), jnp.float32)],
        compiler_params=pltpu.CompilerParams(vmem_limit_bytes=32 * 2**20),
        cost_estimate=pl.CostEstimate(
            flops=6 * 2 * ROWS * BLK * width,
            bytes_accessed=8 * 2**20,
            transcendentals=ROWS * BLK * (width // HD),
        ),
        name="attend",
    )(info, queries, keys, values, grad_out, prev, next_, prev, next_, summary, taps)


def spread(block, axes, count):
    return lax.all_to_all(
        jnp.broadcast_to(block[None], (count,) + block.shape), axes, 0, 0, tiled=True
    )


def per_device(query_rows, key_rows, value_rows, grad_out, conv_weight, frames, window_links):
    queries, keys, values, grad = query_rows[0], key_rows[0], value_rows[0], grad_out[0]
    device = lax.axis_index(TM)
    z_half = lax.axis_index("zh")
    last = lax.axis_size(TM) - 1
    upward = [(i, i + 1) for i in range(last)]
    downward = [(i + 1, i) for i in range(last)]
    swap = [(0, 1), (1, 0)]
    first = device * BLK
    links = window_links[0, 0]
    info = jnp.stack(
        [
            first,
            frames[0],
            jnp.where(device > 0, links[0], 0),
            jnp.where(device < last, links[1], 0),
            z_half,
        ]
    ).astype(jnp.int32)

    packed, own_summary = pack(info, keys, values, grad)
    other_summary = lax.ppermute(own_summary, "zh", swap)
    prev = lax.ppermute(packed, TM, upward)
    next_ = lax.ppermute(packed, TM, downward)
    summary = spread(jnp.concatenate([own_summary, other_summary], axis=1), PLANE, 16)

    dq, center, to_prev, to_next, dsum, conv = attend(
        info, queries, keys, values, grad, prev, next_, summary, conv_weight
    )
    from_prev = lax.ppermute(to_next, TM, upward)
    from_next = lax.ppermute(to_prev, TM, downward)

    dsum = lax.all_to_all(dsum, PLANE, 0, 0, tiled=True)
    dsum = jnp.sum(dsum.astype(jnp.float32), axis=0)
    other = lax.ppermute(dsum[:, SUMM:].astype(jnp.bfloat16), "zh", swap)
    dsum = dsum[:, :SUMM] + other.astype(jnp.float32)

    tap = lax.all_to_all(conv[:, None], PLANE, 0, 0, tiled=True)
    tap = jnp.sum(tap, axis=0)
    tap = jnp.sum(spread(tap, LINE, 32), axis=0)
    taps = spread(tap, PLANE, 16)[:KW, 0]

    row = first + jnp.arange(BLK, dtype=jnp.int32)
    valid = (row < frames[0]).astype(jnp.float32).reshape(SUMM, POOL)
    share = valid / jnp.maximum(jnp.sum(valid, axis=1, keepdims=True), 1.0)
    spread_sum = (dsum[:, :, None] * share[None, :, :, None]).reshape(center.shape)
    total = center + from_prev.astype(jnp.float32) + from_next.astype(jnp.float32)
    total = (total + spread_sum).astype(jnp.bfloat16)
    return dq[None], total[0][None], total[1][None], taps


def solution(mesh):
    names, sizes = zip(*AXES, strict=True)
    fine = Mesh(mesh.devices.reshape(sizes), names)
    rows = P(DP, TM, None)
    return jax.shard_map(
        per_device,
        mesh=fine,
        in_specs=(rows, rows, rows, rows, P(), P(DP), rows),
        out_specs=(rows, rows, rows, P()),
        check_vma=False,
    )
```

```python
import jax
import jax.numpy as jnp
from jax import lax
from jax.experimental import pallas as pl
from jax.experimental.pallas import tpu as pltpu
from jax.sharding import Mesh
from jax.sharding import PartitionSpec as P

H = 8
HD = 128
BLK = 128
POOL = 16
SUMM = BLK // POOL
KW = 9
HALF = 4
WIN = 3 * BLK
ROWS = WIN + 256
SCALE = HD ** (-0.5)
MASKED = -1e30
VMEM = 56 * 2**20
AXES = (("zl", 8), ("core", 2), ("y", 4), ("zh", 2), ("x", 4))
DP = ("zl", "core")
TM = ("y", "zh", "x")
PLANE = ("y", "x")
LINE = ("zl", "core", "zh")


def place():
    z_half = lax.axis_index("zh")
    return (lax.axis_index("y") * 2 + z_half) * 4 + lax.axis_index("x"), z_half


def pack_kernel(frames, k_ref, v_ref, go_ref, packed_ref, summary_ref):
    first, frame_count = place()[0] * BLK, frames[0]
    row = first + lax.broadcasted_iota(jnp.int32, (BLK, 1), 0)
    grad = go_ref[...].astype(jnp.float32)
    grad = jnp.where(row < frame_count, grad, 0.0)
    packed_ref[:BLK, :] = k_ref[...]
    rims = jnp.concatenate([grad[BLK - HALF :], grad[:HALF]], axis=0)
    packed_ref[BLK:, :] = rims.astype(jnp.bfloat16)
    pool = lax.broadcasted_iota(jnp.int32, (SUMM, 1, 1), 0) * POOL + first
    count = jnp.clip(frame_count - pool, 0, POOL)
    frame = pool + lax.broadcasted_iota(jnp.int32, (SUMM, POOL, 1), 1)
    share = jnp.where(
        frame < frame_count, 1.0 / jnp.maximum(count, 1).astype(jnp.float32), 0.0
    )
    for side, ref in ((0, k_ref), (1, v_ref)):
        rows = ref[...].astype(jnp.float32).reshape(SUMM, POOL, ref.shape[1])
        summary_ref[side] = jnp.sum(rows * share, axis=1).astype(jnp.bfloat16)


def pack(frames, keys, values, grad_out):
    width = keys.shape[1]
    chunk = 256
    own = pl.BlockSpec((BLK, chunk), lambda c: (0, c))
    return pl.pallas_call(
        pack_kernel,
        grid=(width // chunk,),
        out_shape=(
            jax.ShapeDtypeStruct((BLK + 8, width), jnp.bfloat16),
            jax.ShapeDtypeStruct((2, SUMM, width), jnp.bfloat16),
        ),
        in_specs=[pl.BlockSpec(memory_space=pltpu.SMEM), own, own, own],
        out_specs=(
            pl.BlockSpec((BLK + 8, chunk), lambda c: (0, c)),
            pl.BlockSpec((2, SUMM, chunk), lambda c: (0, 0, c)),
        ),
        compiler_params=pltpu.CompilerParams(vmem_limit_bytes=VMEM),
        name="pack",
    )(frames, keys, values, grad_out)


def dot(left, right, contract):
    return lax.dot_general(
        left, right, (contract, ((), ())), preferred_element_type=jnp.float32
    )


NN = ((1,), (0,))
NT = ((1,), (1,))
TN = ((0,), (0,))


def attend_kernel(
    frames,
    links,
    q_ref,
    k_ref,
    v_ref,
    go_ref,
    up_k_ref,
    down_k_ref,
    cross_k_ref,
    up_v_ref,
    down_v_ref,
    cross_v_ref,
    up_go_ref,
    down_go_ref,
    cross_go_ref,
    summary_ref,
    w_ref,
    dq_ref,
    center_ref,
    to_prev_ref,
    to_next_ref,
    cross_dk_ref,
    cross_dv_ref,
    dsum_ref,
    conv_ref,
    bias_ref,
):
    device, z_half = place()
    first, frame_count = device * BLK, frames[0]

    @pl.when(pl.program_id(0) == 0)
    def _():
        row = lax.broadcasted_iota(jnp.int32, (BLK, HD), 0)
        seen_left = jnp.where((links[0] == 1) & (device > 0), frame_count - first + BLK, 0)
        seen_right = jnp.where(links[1] == 1, frame_count - first - BLK, 0)
        for part, seen in enumerate((seen_left, frame_count - first, seen_right)):
            bias_ref[pl.ds(part * BLK, BLK), :] = jnp.where(row < seen, 0.0, MASKED)
        row = lax.broadcasted_iota(jnp.int32, (ROWS - WIN, HD), 0)
        source, half, pool = row >> 4, (row >> 3) & 1, row & 7
        block = ((source >> 2) * 2 + (half ^ z_half)) * 4 + (source & 3)
        start = (block * SUMM + pool) * POOL
        bias_ref[WIN:, :] = jnp.where(start < frame_count, 0.0, MASKED)

    x = lax.axis_index("x")
    low, high = x == 0, x == 3
    summary = summary_ref[...]

    def window(up_ref, own_ref, down_ref, cross_ref):
        cross = cross_ref[...]
        return [
            jnp.where(low, cross, up_ref[...]),
            own_ref[...],
            jnp.where(high, cross, down_ref[...]),
        ]

    keys = jnp.concatenate(
        window(up_k_ref, k_ref, down_k_ref, cross_k_ref) + [summary[:, 0].reshape(-1, HD)],
        axis=0,
    )
    values = jnp.concatenate(
        window(up_v_ref, v_ref, down_v_ref, cross_v_ref) + [summary[:, 1].reshape(-1, HD)],
        axis=0,
    )
    queries = q_ref[...]

    row = first + lax.broadcasted_iota(jnp.int32, (BLK, 1), 0)
    grad = jnp.where(row < frame_count, go_ref[...].astype(jnp.float32), 0.0)
    cross_go = cross_go_ref[...].astype(jnp.float32)
    before = jnp.where(low, cross_go, up_go_ref[...].astype(jnp.float32))
    after = jnp.where(high, cross_go, down_go_ref[...].astype(jnp.float32))
    reach = jnp.concatenate([before[:HALF], grad, after[HALF:]], axis=0)
    shifted = [reach[2 * HALF - j : 2 * HALF - j + BLK] for j in range(KW)]
    total = grad
    for j in range(KW):
        total = total + w_ref[j : j + 1, :] * shifted[j]
    grad_attn = total.astype(jnp.bfloat16)

    scores = dot(keys, queries, NT) * SCALE + bias_ref[...]
    top = jnp.max(scores, axis=0, keepdims=True)
    weight = jnp.exp(scores - top)
    prob = weight * (1.0 / jnp.sum(weight, axis=0, keepdims=True))
    prob_bf = prob.astype(jnp.bfloat16)
    attn = dot(prob_bf, values, TN).astype(jnp.bfloat16).astype(jnp.float32)
    delta = jnp.sum(
        (grad_attn.astype(jnp.float32) * attn).T, axis=0, keepdims=True
    )
    dprob = dot(values, grad_attn, NT)
    dscore = (prob * (dprob - delta)).astype(jnp.bfloat16)

    dq_ref[...] = (dot(dscore, keys, TN) * SCALE).astype(jnp.bfloat16)
    for side, part, cross_ref in (
        (0, dot(dscore, queries, NN) * SCALE, cross_dk_ref),
        (1, dot(prob_bf, grad_attn, NN), cross_dv_ref),
    ):
        to_prev_ref[side] = part[:BLK].astype(jnp.bfloat16)
        center_ref[side] = part[BLK : 2 * BLK]
        to_next_ref[side] = part[2 * BLK : WIN].astype(jnp.bfloat16)
        cross_ref[...] = jnp.where(high, part[2 * BLK : WIN], part[:BLK]).astype(jnp.bfloat16)
        dsum_ref[:, side] = (
            part[WIN:].astype(jnp.bfloat16).reshape(dsum_ref.shape[0], 2 * SUMM, HD)
        )
    conv_ref[...] = jnp.concatenate(
        [jnp.sum(attn * shifted[j], axis=0, keepdims=True) for j in range(KW)]
        + [jnp.zeros((16 - KW, HD), jnp.float32)],
        axis=0,
    )


def attend(frames, links, queries, keys, values, grad_out, halo_k, halo_v, summary, taps):
    width = queries.shape[1]
    smem = pl.BlockSpec(memory_space=pltpu.SMEM)
    own = pl.BlockSpec((BLK, HD), lambda h: (0, h))
    pair = pl.BlockSpec((2, BLK, HD), lambda h: (0, 0, h))
    many = pl.BlockSpec((16, 2, 2 * SUMM, HD), lambda h: (0, 0, 0, h))
    rim = pl.BlockSpec((8, HD), lambda h: (BLK // 8, h))
    return pl.pallas_call(
        attend_kernel,
        grid=(width // HD,),
        out_shape=(
            jax.ShapeDtypeStruct((BLK, width), jnp.bfloat16),
            jax.ShapeDtypeStruct((2, BLK, width), jnp.float32),
            jax.ShapeDtypeStruct((2, BLK, width), jnp.bfloat16),
            jax.ShapeDtypeStruct((2, BLK, width), jnp.bfloat16),
            jax.ShapeDtypeStruct((BLK, width), jnp.bfloat16),
            jax.ShapeDtypeStruct((BLK, width), jnp.bfloat16),
            jax.ShapeDtypeStruct((16, 2, 2 * SUMM, width), jnp.bfloat16),
            jax.ShapeDtypeStruct((16, width), jnp.float32),
        ),
        in_specs=[smem, smem]
        + [own] * 10
        + [rim] * 3
        + [many, pl.BlockSpec((KW, HD), lambda h: (0, h))],
        out_specs=(
            own,
            pair,
            pair,
            pair,
            own,
            own,
            many,
            pl.BlockSpec((16, HD), lambda h: (0, h)),
        ),
        scratch_shapes=[pltpu.VMEM((ROWS, HD), jnp.float32)],
        compiler_params=pltpu.CompilerParams(vmem_limit_bytes=VMEM),
        cost_estimate=pl.CostEstimate(
            flops=6 * 2 * ROWS * BLK * width,
            bytes_accessed=8 * 2**20,
            transcendentals=ROWS * BLK * (width // HD),
        ),
        name="attend",
    )(
        frames, links, queries, keys, values, grad_out, *halo_k, *halo_v, *halo_k, summary, taps
    )


def spread(block, axes, count):
    return lax.all_to_all(
        jnp.broadcast_to(block[None], (count,) + block.shape), axes, 0, 0, tiled=True
    )


def fenced(there, step, *operands):
    shapes = jax.eval_shape(step, *operands)
    return lax.cond(
        there,
        step,
        lambda *_: jax.tree.map(lambda leaf: jnp.zeros(leaf.shape, leaf.dtype), shapes),
        *operands,
    )


def routes():
    rows, width = 8, 4
    up, down, diagonal, outward, inward = [], [], [], [], []
    for row in range(rows):
        at = [row * width + x for x in range(width)]
        up += [(at[x], at[x + 1]) for x in range(width - 1)]
        down += [(at[x + 1], at[x]) for x in range(width - 1)]
        inward += [(at[3], at[2]), (at[0], at[1])]
        outward += [(at[2], at[3]), (at[1], at[0])]
        if row + 1 < rows:
            for ours, theirs in ((at[3], at[3] + 1), (at[2], at[3] + 2)):
                diagonal += [(ours, theirs), (theirs, ours)]
    return up, down, diagonal, outward, inward


def per_device(query_rows, key_rows, value_rows, grad_out, conv_weight, frames, window_links):
    queries, keys, values, grad = query_rows[0], key_rows[0], value_rows[0], grad_out[0]
    up, down, diagonal, outward, inward = routes()
    swap = [(0, 1), (1, 0)]
    x = lax.axis_index("x")
    edge = (x == 0) | (x == 3)
    links = window_links[0, 0]
    there = frames[0] > 0

    up_v = lax.ppermute(values, TM, up)
    down_v = lax.ppermute(values, TM, down)
    packed, own_summary = pack(frames, keys, values, grad)
    other_summary = lax.ppermute(own_summary, "zh", swap)
    up_k = lax.ppermute(packed, TM, up)
    down_k = lax.ppermute(packed, TM, down)
    relay = jnp.pad(jnp.where(x == 1, up_v, down_v), ((0, 8), (0, 0)))
    crossing = jnp.where(edge, packed, relay)
    crossing, other_summary = lax.optimization_barrier((crossing, other_summary))
    cross_k = lax.ppermute(crossing, TM, diagonal)
    summary = fenced(
        there,
        lambda own, other: spread(jnp.concatenate([own, other], axis=1), PLANE, 16),
        own_summary,
        other_summary,
    )
    cross_k, summary = lax.optimization_barrier((cross_k, summary))
    cross_v = lax.ppermute(cross_k[:BLK], TM, outward)

    dq, center, to_prev, to_next, cross_dk, cross_dv, dsum, conv = attend(
        frames,
        links,
        queries,
        keys,
        values,
        grad,
        (up_k, down_k, cross_k),
        (up_v, down_v, cross_v),
        summary,
        conv_weight,
    )

    from_prev = lax.ppermute(to_next, TM, up)
    from_next = lax.ppermute(to_prev, TM, down)
    relay = lax.ppermute(cross_dv, TM, inward)

    def to_owners(dsum, conv):
        dsum = lax.all_to_all(dsum, PLANE, 0, 0, tiled=True)
        tap = lax.all_to_all(conv[:, None], PLANE, 0, 0, tiled=True)
        return jnp.sum(dsum.astype(jnp.float32), axis=0), jnp.sum(tap, axis=0)

    dsum, tap = fenced(there, to_owners, dsum, conv)
    relay, dsum, tap = lax.optimization_barrier((relay, dsum, tap))
    cross_dk = lax.ppermute(jnp.where(edge, cross_dk, relay), TM, diagonal)

    def along_line(dsum, tap):
        other = lax.ppermute(dsum[:, SUMM:].astype(jnp.bfloat16), "zh", swap)
        tap = jnp.sum(spread(tap, LINE, 32), axis=0)
        return dsum[:, :SUMM] + other.astype(jnp.float32), tap

    dsum, tap = fenced(there, along_line, dsum, tap)
    cross_dk, dsum, tap = lax.optimization_barrier((cross_dk, dsum, tap))
    cross_dv = lax.ppermute(cross_dk, TM, outward)
    taps = spread(tap, PLANE, 16)[:KW, 0]

    row = lax.axis_index(TM) * BLK + jnp.arange(BLK, dtype=jnp.int32)
    valid = (row < frames[0]).astype(jnp.float32).reshape(SUMM, POOL)
    share = valid / jnp.maximum(jnp.sum(valid, axis=1, keepdims=True), 1.0)

    def total(side, cross):
        spread_sum = (dsum[side][:, None] * share[:, :, None]).reshape(center[side].shape)
        near = from_prev[side].astype(jnp.float32) + from_next[side].astype(jnp.float32)
        far = jnp.where(edge, cross.astype(jnp.float32), 0.0)
        return (center[side] + near + far + spread_sum).astype(jnp.bfloat16)[None]

    return dq[None], total(0, cross_dk), total(1, cross_dv), taps


def solution(mesh):
    names, sizes = zip(*AXES, strict=True)
    fine = Mesh(mesh.devices.reshape(sizes), names)
    rows = P(DP, TM, None)
    return jax.shard_map(
        per_device,
        mesh=fine,
        in_specs=(rows, rows, rows, rows, P(), P(DP), rows),
        out_specs=(rows, rows, rows, P()),
        check_vma=False,
    )
```

```python
import jax
import jax.numpy as jnp
from jax import lax
from jax.experimental import pallas as pl
from jax.experimental.pallas import tpu as pltpu
from jax.sharding import Mesh
from jax.sharding import PartitionSpec as P

H = 8
HD = 128
HEADS = 4
BLK = 128
POOL = 16
SUMM = BLK // POOL
KW = 9
HALF = 4
WIN = 3 * BLK
ROWS = WIN + 256
SCALE = HD ** (-0.5)
MASKED = -1e30
VMEM = 56 * 2**20
AXES = (("zl", 8), ("core", 2), ("y", 4), ("zh", 2), ("x", 4))
DP = ("zl", "core")
TM = ("y", "zh", "x")
PLANE = ("y", "x")
LINE = ("zl", "core", "zh")


def place():
    z_half = lax.axis_index("zh")
    return (lax.axis_index("y") * 2 + z_half) * 4 + lax.axis_index("x"), z_half


def pack_kernel(frames, k_ref, v_ref, go_ref, packed_ref, summary_ref):
    first, frame_count = place()[0] * BLK, frames[0]
    row = first + lax.broadcasted_iota(jnp.int32, (BLK, 1), 0)
    grad = go_ref[...].astype(jnp.float32)
    grad = jnp.where(row < frame_count, grad, 0.0)
    packed_ref[:BLK, :] = k_ref[...]
    rims = jnp.concatenate([grad[BLK - HALF :], grad[:HALF]], axis=0)
    packed_ref[BLK:, :] = rims.astype(jnp.bfloat16)
    pool = lax.broadcasted_iota(jnp.int32, (SUMM, 1, 1), 0) * POOL + first
    count = jnp.clip(frame_count - pool, 0, POOL)
    frame = pool + lax.broadcasted_iota(jnp.int32, (SUMM, POOL, 1), 1)
    share = jnp.where(
        frame < frame_count, 1.0 / jnp.maximum(count, 1).astype(jnp.float32), 0.0
    )
    for side, ref in ((0, k_ref), (1, v_ref)):
        rows = ref[...].astype(jnp.float32).reshape(SUMM, POOL, ref.shape[1])
        summary_ref[side] = jnp.sum(rows * share, axis=1).astype(jnp.bfloat16)


def pack(frames, keys, values, grad_out):
    width = keys.shape[1]
    chunk = 256
    own = pl.BlockSpec((BLK, chunk), lambda c: (0, c))
    return pl.pallas_call(
        pack_kernel,
        grid=(width // chunk,),
        out_shape=(
            jax.ShapeDtypeStruct((BLK + 8, width), jnp.bfloat16),
            jax.ShapeDtypeStruct((2, SUMM, width), jnp.bfloat16),
        ),
        in_specs=[pl.BlockSpec(memory_space=pltpu.SMEM), own, own, own],
        out_specs=(
            pl.BlockSpec((BLK + 8, chunk), lambda c: (0, c)),
            pl.BlockSpec((2, SUMM, chunk), lambda c: (0, 0, c)),
        ),
        compiler_params=pltpu.CompilerParams(vmem_limit_bytes=VMEM),
        name="pack",
    )(frames, keys, values, grad_out)


def dot(left, right, contract):
    return lax.dot_general(
        left, right, (contract, ((), ())), preferred_element_type=jnp.float32
    )


NN = ((1,), (0,))
NT = ((1,), (1,))
TN = ((0,), (0,))


def attend_kernel(
    frames,
    links,
    q_ref,
    k_ref,
    v_ref,
    go_ref,
    up_k_ref,
    down_k_ref,
    cross_k_ref,
    up_v_ref,
    down_v_ref,
    cross_v_ref,
    up_go_ref,
    down_go_ref,
    cross_go_ref,
    summary_ref,
    w_ref,
    dq_ref,
    center_ref,
    to_prev_ref,
    to_next_ref,
    cross_dk_ref,
    cross_dv_ref,
    dsum_ref,
    bias_ref,
):
    device, z_half = place()
    first, frame_count = device * BLK, frames[0]

    @pl.when(pl.program_id(0) == 0)
    def _():
        row = lax.broadcasted_iota(jnp.int32, (BLK, HD), 0)
        seen_left = jnp.where((links[0] == 1) & (device > 0), frame_count - first + BLK, 0)
        seen_right = jnp.where(links[1] == 1, frame_count - first - BLK, 0)
        for part, seen in enumerate((seen_left, frame_count - first, seen_right)):
            bias_ref[pl.ds(part * BLK, BLK), :] = jnp.where(row < seen, 0.0, MASKED)
        row = lax.broadcasted_iota(jnp.int32, (ROWS - WIN, HD), 0)
        source, half, pool = row >> 4, (row >> 3) & 1, row & 7
        block = ((source >> 2) * 2 + (half ^ z_half)) * 4 + (source & 3)
        start = (block * SUMM + pool) * POOL
        bias_ref[WIN:, :] = jnp.where(start < frame_count, 0.0, MASKED)

    x = lax.axis_index("x")
    low, high = x == 0, x == 3

    def one_head(c):

        def window(up_ref, own_ref, down_ref, cross_ref):
            cross = cross_ref[:BLK, c]
            return [
                jnp.where(low, cross, up_ref[:BLK, c]),
                own_ref[:, c],
                jnp.where(high, cross, down_ref[:, c]),
            ]

        keys = jnp.concatenate(
            window(up_k_ref, k_ref, down_k_ref, cross_k_ref) + [summary_ref[:, 0, :, c].reshape(-1, HD)],
            axis=0,
        )
        values = jnp.concatenate(
            window(up_v_ref, v_ref, down_v_ref, cross_v_ref) + [summary_ref[:, 1, :, c].reshape(-1, HD)],
            axis=0,
        )
        queries = q_ref[:, c]

        row = first + lax.broadcasted_iota(jnp.int32, (BLK, 1), 0)
        grad = jnp.where(row < frame_count, go_ref[:, c].astype(jnp.float32), 0.0)
        cross_go = cross_go_ref[:, c].astype(jnp.float32)
        before = jnp.where(low, cross_go, up_go_ref[:, c].astype(jnp.float32))
        after = jnp.where(high, cross_go, down_go_ref[:, c].astype(jnp.float32))
        reach = jnp.concatenate([before[:HALF], grad, after[HALF:]], axis=0)
        shifted = [reach[2 * HALF - j : 2 * HALF - j + BLK] for j in range(KW)]
        total = grad
        for j in range(KW):
            total = total + w_ref[j : j + 1, c] * shifted[j]
        grad_attn = total.astype(jnp.bfloat16)

        scores = dot(keys, queries, NT) * SCALE + bias_ref[...]
        top = jnp.max(scores, axis=0, keepdims=True)
        weight = jnp.exp(scores - top)
        prob = weight * (1.0 / jnp.sum(weight, axis=0, keepdims=True))
        prob_bf = prob.astype(jnp.bfloat16)
        attn = dot(prob_bf, values, TN).astype(jnp.bfloat16).astype(jnp.float32)
        delta = jnp.sum(
            (grad_attn.astype(jnp.float32) * attn).T, axis=0, keepdims=True
        )
        dprob = dot(values, grad_attn, NT)
        dscore = (prob * (dprob - delta)).astype(jnp.bfloat16)

        dq_ref[:, c] = (dot(dscore, keys, TN) * SCALE).astype(jnp.bfloat16)
        for side, part, cross_ref in (
            (0, dot(dscore, queries, NN) * SCALE, cross_dk_ref),
            (1, dot(prob_bf, grad_attn, NN), cross_dv_ref),
        ):
            to_prev_ref[side, :, c] = part[:BLK].astype(jnp.bfloat16)
            center_ref[side, :, c] = part[BLK : 2 * BLK]
            to_next_ref[side, :, c] = part[2 * BLK : WIN].astype(jnp.bfloat16)
            cross_ref[:, c] = jnp.where(high, part[2 * BLK : WIN], part[:BLK]).astype(jnp.bfloat16)
            dsum_ref[:, side, : 2 * SUMM, c] = (
                part[WIN:].astype(jnp.bfloat16).reshape(dsum_ref.shape[0], 2 * SUMM, HD)
            )
        empty = jnp.zeros((SUMM, HD), jnp.float32)
        for j in range(16):
            if j < KW:
                tap = jnp.sum(attn * shifted[j], axis=0, keepdims=True)
                big = tap.astype(jnp.bfloat16).astype(jnp.float32)
                terms = (big + empty, (tap - big) + empty)
            else:
                terms = (empty, empty)
            for side, term in enumerate(terms):
                dsum_ref[j, side, 2 * SUMM :, c] = term.astype(jnp.bfloat16)

    for head in range(HEADS):
        one_head(slice(head * HD, (head + 1) * HD))


def attend(frames, links, queries, keys, values, grad_out, halo_k, halo_v, summary, taps):
    width = queries.shape[1]
    step = HEADS * HD
    smem = pl.BlockSpec(memory_space=pltpu.SMEM)
    own = pl.BlockSpec((BLK, step), lambda h: (0, h))
    pair = pl.BlockSpec((2, BLK, step), lambda h: (0, 0, h))
    many = pl.BlockSpec((16, 2, 2 * SUMM, step), lambda h: (0, 0, 0, h))
    rim = pl.BlockSpec((8, step), lambda h: (BLK // 8, h))
    return pl.pallas_call(
        attend_kernel,
        grid=(width // step,),
        out_shape=(
            jax.ShapeDtypeStruct((BLK, width), jnp.bfloat16),
            jax.ShapeDtypeStruct((2, BLK, width), jnp.float32),
            jax.ShapeDtypeStruct((2, BLK, width), jnp.bfloat16),
            jax.ShapeDtypeStruct((2, BLK, width), jnp.bfloat16),
            jax.ShapeDtypeStruct((BLK, width), jnp.bfloat16),
            jax.ShapeDtypeStruct((BLK, width), jnp.bfloat16),
            jax.ShapeDtypeStruct((16, 2, 3 * SUMM, width), jnp.bfloat16),
        ),
        in_specs=[smem, smem]
        + [own] * 10
        + [rim] * 3
        + [many, pl.BlockSpec((KW, step), lambda h: (0, h))],
        out_specs=(
            own,
            pair,
            pair,
            pair,
            own,
            own,
            pl.BlockSpec((16, 2, 3 * SUMM, step), lambda h: (0, 0, 0, h)),
        ),
        scratch_shapes=[pltpu.VMEM((ROWS, HD), jnp.float32)],
        compiler_params=pltpu.CompilerParams(vmem_limit_bytes=VMEM),
        cost_estimate=pl.CostEstimate(
            flops=6 * 2 * ROWS * BLK * width,
            bytes_accessed=8 * 2**20,
            transcendentals=ROWS * BLK * (width // HD),
        ),
        name="attend",
    )(
        frames, links, queries, keys, values, grad_out, *halo_k, *halo_v, *halo_k, summary, taps
    )


def spread(block, axes, count):
    return lax.all_to_all(
        jnp.broadcast_to(block[None], (count,) + block.shape), axes, 0, 0, tiled=True
    )


def fenced(there, step, *operands):
    shapes = jax.eval_shape(step, *operands)
    return lax.cond(
        there,
        step,
        lambda *_: jax.tree.map(lambda leaf: jnp.zeros(leaf.shape, leaf.dtype), shapes),
        *operands,
    )


def routes():
    rows, width = 8, 4
    up, down, diagonal, outward, inward = [], [], [], [], []
    for row in range(rows):
        at = [row * width + x for x in range(width)]
        up += [(at[x], at[x + 1]) for x in range(width - 1)]
        down += [(at[x + 1], at[x]) for x in range(width - 1)]
        inward += [(at[3], at[2]), (at[0], at[1])]
        outward += [(at[2], at[3]), (at[1], at[0])]
        if row + 1 < rows:
            for ours, theirs in ((at[3], at[3] + 1), (at[2], at[3] + 2)):
                diagonal += [(ours, theirs), (theirs, ours)]
    return up, down, diagonal, outward, inward


def per_device(query_rows, key_rows, value_rows, grad_out, conv_weight, frames, window_links):
    queries, keys, values, grad = query_rows[0], key_rows[0], value_rows[0], grad_out[0]
    up, down, diagonal, outward, inward = routes()
    swap = [(0, 1), (1, 0)]
    x = lax.axis_index("x")
    edge = (x == 0) | (x == 3)
    links = window_links[0, 0]
    there = frames[0] > 0

    up_v = lax.ppermute(values, TM, up)
    down_v = lax.ppermute(values, TM, down)
    packed, own_summary = pack(frames, keys, values, grad)
    other_summary = lax.ppermute(own_summary, "zh", swap)
    up_k = lax.ppermute(packed, TM, up)
    down_k = lax.ppermute(packed, TM, down)
    relay = jnp.pad(jnp.where(x == 1, up_v, down_v), ((0, 8), (0, 0)))
    crossing = jnp.where(edge, packed, relay)
    crossing, other_summary = lax.optimization_barrier((crossing, other_summary))
    cross_k = lax.ppermute(crossing, TM, diagonal)
    summary = fenced(
        there,
        lambda own, other: spread(jnp.concatenate([own, other], axis=1), PLANE, 16),
        own_summary,
        other_summary,
    )
    cross_k, summary = lax.optimization_barrier((cross_k, summary))
    cross_v = lax.ppermute(cross_k[:BLK], TM, outward)

    dq, center, to_prev, to_next, cross_dk, cross_dv, dsum = attend(
        frames,
        links,
        queries,
        keys,
        values,
        grad,
        (up_k, down_k, cross_k),
        (up_v, down_v, cross_v),
        summary,
        conv_weight,
    )

    from_prev = lax.ppermute(to_next, TM, up)
    from_next = lax.ppermute(to_prev, TM, down)
    relay = lax.ppermute(cross_dv, TM, inward)

    relay, dsum = lax.optimization_barrier((relay, dsum))
    dsum = lax.all_to_all(dsum, PLANE, 0, 0, tiled=True)
    dsum = jnp.sum(dsum.astype(jnp.float32), axis=0)
    tap = dsum[0, 2 * SUMM : 2 * SUMM + 1] + dsum[1, 2 * SUMM : 2 * SUMM + 1]
    cross_dk = lax.ppermute(jnp.where(edge, cross_dk, relay), TM, diagonal)

    tap = fenced(there, lambda tap: jnp.sum(spread(tap, LINE, 32), axis=0), tap)
    cross_dk, dsum, tap = lax.optimization_barrier((cross_dk, dsum, tap))
    cross_dv = lax.ppermute(cross_dk, TM, outward)
    taps = spread(tap, PLANE, 16)[:KW, 0]
    other = lax.ppermute(dsum[:, SUMM : 2 * SUMM].astype(jnp.bfloat16), "zh", swap)
    dsum = dsum[:, :SUMM] + other.astype(jnp.float32)

    row = lax.axis_index(TM) * BLK + jnp.arange(BLK, dtype=jnp.int32)
    valid = (row < frames[0]).astype(jnp.float32).reshape(SUMM, POOL)
    share = valid / jnp.maximum(jnp.sum(valid, axis=1, keepdims=True), 1.0)

    def total(side, cross):
        spread_sum = (dsum[side][:, None] * share[:, :, None]).reshape(center[side].shape)
        near = from_prev[side].astype(jnp.float32) + from_next[side].astype(jnp.float32)
        far = jnp.where(edge, cross.astype(jnp.float32), 0.0)
        return (center[side] + near + far + spread_sum).astype(jnp.bfloat16)[None]

    return dq[None], total(0, cross_dk), total(1, cross_dv), taps


def solution(mesh):
    names, sizes = zip(*AXES, strict=True)
    fine = Mesh(mesh.devices.reshape(sizes), names)
    rows = P(DP, TM, None)
    return jax.shard_map(
        per_device,
        mesh=fine,
        in_specs=(rows, rows, rows, rows, P(), P(DP), rows),
        out_specs=(rows, rows, rows, P()),
        check_vma=False,
    )
```

```python
import jax
import jax.numpy as jnp
from jax import lax
from jax.experimental import pallas as pl
from jax.experimental.pallas import tpu as pltpu
from jax.sharding import Mesh
from jax.sharding import PartitionSpec as P

H = 8
HD = 128
HEADS = 4
BLK = 128
POOL = 16
SUMM = BLK // POOL
KW = 9
HALF = 4
WIN = 3 * BLK
ROWS = WIN + 256
SCALE = HD ** (-0.5)
MASKED = -1e30
VMEM = 56 * 2**20
AXES = (("zl", 8), ("core", 2), ("y", 4), ("zh", 2), ("x", 4))
DP = ("zl", "core")
TM = ("y", "zh", "x")
PLANE = ("y", "x")
LINE = ("zl", "core", "zh")


def place():
    z_half = lax.axis_index("zh")
    return (lax.axis_index("y") * 2 + z_half) * 4 + lax.axis_index("x"), z_half


def pack_kernel(frames, k_ref, v_ref, go_ref, packed_ref, summary_ref):
    first, frame_count = place()[0] * BLK, frames[0]
    row = first + lax.broadcasted_iota(jnp.int32, (BLK, 1), 0)
    grad = go_ref[...].astype(jnp.float32)
    grad = jnp.where(row < frame_count, grad, 0.0)
    packed_ref[:BLK, :] = k_ref[...]
    rims = jnp.concatenate([grad[BLK - HALF :], grad[:HALF]], axis=0)
    packed_ref[BLK:, :] = rims.astype(jnp.bfloat16)
    pool = lax.broadcasted_iota(jnp.int32, (SUMM, 1, 1), 0) * POOL + first
    count = jnp.clip(frame_count - pool, 0, POOL)
    frame = pool + lax.broadcasted_iota(jnp.int32, (SUMM, POOL, 1), 1)
    share = jnp.where(
        frame < frame_count, 1.0 / jnp.maximum(count, 1).astype(jnp.float32), 0.0
    )
    for side, ref in ((0, k_ref), (1, v_ref)):
        rows = ref[...].astype(jnp.float32).reshape(SUMM, POOL, ref.shape[1])
        summary_ref[side] = jnp.sum(rows * share, axis=1).astype(jnp.bfloat16)


def pack(frames, keys, values, grad_out):
    width = keys.shape[1]
    chunk = 512
    own = pl.BlockSpec((BLK, chunk), lambda c: (0, c))
    return pl.pallas_call(
        pack_kernel,
        grid=(width // chunk,),
        out_shape=(
            jax.ShapeDtypeStruct((BLK + 8, width), jnp.bfloat16),
            jax.ShapeDtypeStruct((2, SUMM, width), jnp.bfloat16),
        ),
        in_specs=[pl.BlockSpec(memory_space=pltpu.SMEM), own, own, own],
        out_specs=(
            pl.BlockSpec((BLK + 8, chunk), lambda c: (0, c)),
            pl.BlockSpec((2, SUMM, chunk), lambda c: (0, 0, c)),
        ),
        compiler_params=pltpu.CompilerParams(vmem_limit_bytes=VMEM),
        name="pack",
    )(frames, keys, values, grad_out)


def dot(left, right, contract):
    return lax.dot_general(
        left, right, (contract, ((), ())), preferred_element_type=jnp.float32
    )


NN = ((1,), (0,))
NT = ((1,), (1,))
TN = ((0,), (0,))


def attend_kernel(
    frames,
    links,
    q_ref,
    k_ref,
    v_ref,
    go_ref,
    up_k_ref,
    down_k_ref,
    cross_k_ref,
    up_v_ref,
    down_v_ref,
    cross_v_ref,
    up_go_ref,
    down_go_ref,
    cross_go_ref,
    summary_ref,
    w_ref,
    dq_ref,
    center_ref,
    to_prev_ref,
    to_next_ref,
    cross_dk_ref,
    cross_dv_ref,
    dsum_ref,
    bias_ref,
):
    device, z_half = place()
    first, frame_count = device * BLK, frames[0]

    @pl.when(pl.program_id(0) == 0)
    def _():
        row = lax.broadcasted_iota(jnp.int32, (BLK, HD), 0)
        seen_left = jnp.where((links[0] == 1) & (device > 0), frame_count - first + BLK, 0)
        seen_right = jnp.where(links[1] == 1, frame_count - first - BLK, 0)
        for part, seen in enumerate((seen_left, frame_count - first, seen_right)):
            bias_ref[pl.ds(part * BLK, BLK), :] = jnp.where(row < seen, 0.0, MASKED)
        row = lax.broadcasted_iota(jnp.int32, (ROWS - WIN, HD), 0)
        source, half, pool = row >> 4, (row >> 3) & 1, row & 7
        block = ((source >> 2) * 2 + (half ^ z_half)) * 4 + (source & 3)
        start = (block * SUMM + pool) * POOL
        bias_ref[WIN:, :] = jnp.where(start < frame_count, 0.0, MASKED)

    x = lax.axis_index("x")
    low, high = x == 0, x == 3

    def one_head(c):

        def window(up_ref, own_ref, down_ref, cross_ref):
            cross = cross_ref[:BLK, c]
            return [
                jnp.where(low, cross, up_ref[:BLK, c]),
                own_ref[:, c],
                jnp.where(high, cross, down_ref[:, c]),
            ]

        keys = jnp.concatenate(
            window(up_k_ref, k_ref, down_k_ref, cross_k_ref) + [summary_ref[:, 0, :, c].reshape(-1, HD)],
            axis=0,
        )
        values = jnp.concatenate(
            window(up_v_ref, v_ref, down_v_ref, cross_v_ref) + [summary_ref[:, 1, :, c].reshape(-1, HD)],
            axis=0,
        )
        queries = q_ref[:, c]

        row = first + lax.broadcasted_iota(jnp.int32, (BLK, 1), 0)
        grad = jnp.where(row < frame_count, go_ref[:, c].astype(jnp.float32), 0.0)
        cross_go = cross_go_ref[:, c].astype(jnp.float32)
        before = jnp.where(low, cross_go, up_go_ref[:, c].astype(jnp.float32))
        after = jnp.where(high, cross_go, down_go_ref[:, c].astype(jnp.float32))
        reach = jnp.concatenate([before[:HALF], grad, after[HALF:]], axis=0)
        shifted = [reach[2 * HALF - j : 2 * HALF - j + BLK] for j in range(KW)]
        total = grad
        for j in range(KW):
            total = total + w_ref[j : j + 1, c] * shifted[j]
        grad_attn = total.astype(jnp.bfloat16)

        scores = dot(keys, queries, NT) * SCALE + bias_ref[...]
        top = jnp.max(scores, axis=0, keepdims=True)
        weight = jnp.exp(scores - top)
        prob = weight * (1.0 / jnp.sum(weight, axis=0, keepdims=True))
        prob_bf = prob.astype(jnp.bfloat16)
        attn = dot(prob_bf, values, TN).astype(jnp.bfloat16).astype(jnp.float32)
        delta = jnp.sum(
            (grad_attn.astype(jnp.float32) * attn).T, axis=0, keepdims=True
        )
        dprob = dot(values, grad_attn, NT)
        dscore = (prob * (dprob - delta)).astype(jnp.bfloat16)

        dq_ref[:, c] = (dot(dscore, keys, TN) * SCALE).astype(jnp.bfloat16)
        for side, part, cross_ref in (
            (0, dot(dscore, queries, NN) * SCALE, cross_dk_ref),
            (1, dot(prob_bf, grad_attn, NN), cross_dv_ref),
        ):
            to_prev_ref[side, :, c] = part[:BLK].astype(jnp.bfloat16)
            center_ref[side, :, c] = part[BLK : 2 * BLK]
            to_next_ref[side, :, c] = part[2 * BLK : WIN].astype(jnp.bfloat16)
            cross_ref[:, c] = jnp.where(high, part[2 * BLK : WIN], part[:BLK]).astype(jnp.bfloat16)
            dsum_ref[:, side, : 2 * SUMM, c] = (
                part[WIN:].astype(jnp.bfloat16).reshape(dsum_ref.shape[0], 2 * SUMM, HD)
            )
        empty = jnp.zeros((SUMM, HD), jnp.float32)
        for j in range(16):
            if j < KW:
                tap = jnp.sum(attn * shifted[j], axis=0, keepdims=True)
                big = tap.astype(jnp.bfloat16).astype(jnp.float32)
                terms = (big + empty, (tap - big) + empty)
            else:
                terms = (empty, empty)
            for side, term in enumerate(terms):
                dsum_ref[j, side, 2 * SUMM :, c] = term.astype(jnp.bfloat16)

    for head in range(HEADS):
        one_head(slice(head * HD, (head + 1) * HD))


def attend(frames, links, queries, keys, values, grad_out, halo_k, halo_v, summary, taps):
    width = queries.shape[1]
    step = HEADS * HD
    smem = pl.BlockSpec(memory_space=pltpu.SMEM)
    own = pl.BlockSpec((BLK, step), lambda h: (0, h))
    pair = pl.BlockSpec((2, BLK, step), lambda h: (0, 0, h))
    many = pl.BlockSpec((16, 2, 2 * SUMM, step), lambda h: (0, 0, 0, h))
    rim = pl.BlockSpec((8, step), lambda h: (BLK // 8, h))
    return pl.pallas_call(
        attend_kernel,
        grid=(width // step,),
        out_shape=(
            jax.ShapeDtypeStruct((BLK, width), jnp.bfloat16),
            jax.ShapeDtypeStruct((2, BLK, width), jnp.float32),
            jax.ShapeDtypeStruct((2, BLK, width), jnp.bfloat16),
            jax.ShapeDtypeStruct((2, BLK, width), jnp.bfloat16),
            jax.ShapeDtypeStruct((BLK, width), jnp.bfloat16),
            jax.ShapeDtypeStruct((BLK, width), jnp.bfloat16),
            jax.ShapeDtypeStruct((16, 2, 3 * SUMM, width), jnp.bfloat16),
        ),
        in_specs=[smem, smem]
        + [own] * 10
        + [rim] * 3
        + [many, pl.BlockSpec((KW, step), lambda h: (0, h))],
        out_specs=(
            own,
            pair,
            pair,
            pair,
            own,
            own,
            pl.BlockSpec((16, 2, 3 * SUMM, step), lambda h: (0, 0, 0, h)),
        ),
        scratch_shapes=[pltpu.VMEM((ROWS, HD), jnp.float32)],
        compiler_params=pltpu.CompilerParams(vmem_limit_bytes=VMEM),
        cost_estimate=pl.CostEstimate(
            flops=6 * 2 * ROWS * BLK * width,
            bytes_accessed=8 * 2**20,
            transcendentals=ROWS * BLK * (width // HD),
        ),
        name="attend",
    )(
        frames, links, queries, keys, values, grad_out, *halo_k, *halo_v, *halo_k, summary, taps
    )


def spread(block, axes, count):
    return lax.all_to_all(
        jnp.broadcast_to(block[None], (count,) + block.shape), axes, 0, 0, tiled=True
    )


def fenced(there, step, *operands):
    shapes = jax.eval_shape(step, *operands)
    return lax.cond(
        there,
        step,
        lambda *_: jax.tree.map(lambda leaf: jnp.zeros(leaf.shape, leaf.dtype), shapes),
        *operands,
    )


def routes():
    rows, width = 8, 4
    up, down, diagonal, outward, inward = [], [], [], [], []
    for row in range(rows):
        at = [row * width + x for x in range(width)]
        up += [(at[x], at[x + 1]) for x in range(width - 1)]
        down += [(at[x + 1], at[x]) for x in range(width - 1)]
        inward += [(at[3], at[2]), (at[0], at[1])]
        outward += [(at[2], at[3]), (at[1], at[0])]
        if row + 1 < rows:
            for ours, theirs in ((at[3], at[3] + 1), (at[2], at[3] + 2)):
                diagonal += [(ours, theirs), (theirs, ours)]
    return up, down, diagonal, outward, inward


def per_device(query_rows, key_rows, value_rows, grad_out, conv_weight, frames, window_links):
    queries, keys, values, grad = query_rows[0], key_rows[0], value_rows[0], grad_out[0]
    up, down, diagonal, outward, inward = routes()
    swap = [(0, 1), (1, 0)]
    x = lax.axis_index("x")
    edge = (x == 0) | (x == 3)
    links = window_links[0, 0]
    there = frames[0] > 0

    up_v = lax.ppermute(values, TM, up)
    down_v = lax.ppermute(values, TM, down)
    packed, own_summary = pack(frames, keys, values, grad)
    other_summary = lax.ppermute(own_summary, "zh", swap)
    up_k = lax.ppermute(packed, TM, up)
    down_k = lax.ppermute(packed, TM, down)
    relay = jnp.pad(jnp.where(x == 1, up_v, down_v), ((0, 8), (0, 0)))
    crossing = jnp.where(edge, packed, relay)
    crossing, other_summary = lax.optimization_barrier((crossing, other_summary))
    cross_k = lax.ppermute(crossing, TM, diagonal)
    summary = fenced(
        there,
        lambda own, other: spread(jnp.concatenate([own, other], axis=1), PLANE, 16),
        own_summary,
        other_summary,
    )
    cross_k, summary = lax.optimization_barrier((cross_k, summary))
    cross_v = lax.ppermute(cross_k[:BLK], TM, outward)

    dq, center, to_prev, to_next, cross_dk, cross_dv, dsum = attend(
        frames,
        links,
        queries,
        keys,
        values,
        grad,
        (up_k, down_k, cross_k),
        (up_v, down_v, cross_v),
        summary,
        conv_weight,
    )

    from_prev = lax.ppermute(to_next, TM, up)
    from_next = lax.ppermute(to_prev, TM, down)
    relay = lax.ppermute(cross_dv, TM, inward)

    relay, dsum = lax.optimization_barrier((relay, dsum))
    dsum = lax.all_to_all(dsum, PLANE, 0, 0, tiled=True)
    dsum = jnp.sum(dsum.astype(jnp.float32), axis=0)
    tap = dsum[0, 2 * SUMM : 2 * SUMM + 1] + dsum[1, 2 * SUMM : 2 * SUMM + 1]
    cross_dk = lax.ppermute(jnp.where(edge, cross_dk, relay), TM, diagonal)

    tap = fenced(there, lambda tap: jnp.sum(spread(tap, LINE, 32), axis=0), tap)
    cross_dk, dsum, tap = lax.optimization_barrier((cross_dk, dsum, tap))
    cross_dv = lax.ppermute(cross_dk, TM, outward)
    taps = spread(tap, PLANE, 16)[:KW, 0]
    other = lax.ppermute(dsum[:, SUMM : 2 * SUMM].astype(jnp.bfloat16), "zh", swap)
    dsum = dsum[:, :SUMM] + other.astype(jnp.float32)

    row = lax.axis_index(TM) * BLK + jnp.arange(BLK, dtype=jnp.int32)
    valid = (row < frames[0]).astype(jnp.float32).reshape(SUMM, POOL)
    share = valid / jnp.maximum(jnp.sum(valid, axis=1, keepdims=True), 1.0)

    def total(side, cross):
        spread_sum = (dsum[side][:, None] * share[:, :, None]).reshape(center[side].shape)
        near = from_prev[side].astype(jnp.float32) + from_next[side].astype(jnp.float32)
        far = jnp.where(edge, cross.astype(jnp.float32), 0.0)
        return (center[side] + near + far + spread_sum).astype(jnp.bfloat16)[None]

    return dq[None], total(0, cross_dk), total(1, cross_dv), taps


def solution(mesh):
    names, sizes = zip(*AXES, strict=True)
    fine = Mesh(mesh.devices.reshape(sizes), names)
    rows = P(DP, TM, None)
    return jax.shard_map(
        per_device,
        mesh=fine,
        in_specs=(rows, rows, rows, rows, P(), P(DP), rows),
        out_specs=(rows, rows, rows, P()),
        check_vma=False,
    )
```

```python
import jax
import jax.numpy as jnp
from jax import lax
from jax.experimental import pallas as pl
from jax.experimental.pallas import tpu as pltpu
from jax.sharding import Mesh
from jax.sharding import PartitionSpec as P

H = 8
HD = 128
HEADS = 4
BLK = 128
POOL = 16
SUMM = BLK // POOL
KW = 9
HALF = 4
WIN = 3 * BLK
ROWS = WIN + 256
SCALE = HD ** (-0.5)
MASKED = -1e30
VMEM = 56 * 2**20
AXES = (("zl", 8), ("core", 2), ("y", 4), ("zh", 2), ("x", 4))
DP = ("zl", "core")
TM = ("y", "zh", "x")
PLANE = ("y", "x")
LINE = ("zl", "core", "zh")


def place():
    z_half = lax.axis_index("zh")
    return (lax.axis_index("y") * 2 + z_half) * 4 + lax.axis_index("x"), z_half


def pack_kernel(frames, k_ref, v_ref, go_ref, packed_ref, summary_ref):
    first, frame_count = place()[0] * BLK, frames[0]
    row = first + lax.broadcasted_iota(jnp.int32, (BLK, 1), 0)
    grad = go_ref[...].astype(jnp.float32)
    grad = jnp.where(row < frame_count, grad, 0.0)
    packed_ref[:BLK, :] = k_ref[...]
    rims = jnp.concatenate([grad[BLK - HALF :], grad[:HALF]], axis=0)
    packed_ref[BLK:, :] = rims.astype(jnp.bfloat16)
    pool = lax.broadcasted_iota(jnp.int32, (SUMM, 1, 1), 0) * POOL + first
    count = jnp.clip(frame_count - pool, 0, POOL)
    frame = pool + lax.broadcasted_iota(jnp.int32, (SUMM, POOL, 1), 1)
    share = jnp.where(
        frame < frame_count, 1.0 / jnp.maximum(count, 1).astype(jnp.float32), 0.0
    )
    for side, ref in ((0, k_ref), (1, v_ref)):
        rows = ref[...].astype(jnp.float32).reshape(SUMM, POOL, ref.shape[1])
        summary_ref[side] = jnp.sum(rows * share, axis=1).astype(jnp.bfloat16)


def pack(frames, keys, values, grad_out):
    width = keys.shape[1]
    chunk = 512
    own = pl.BlockSpec((BLK, chunk), lambda c: (0, c))
    return pl.pallas_call(
        pack_kernel,
        grid=(width // chunk,),
        out_shape=(
            jax.ShapeDtypeStruct((BLK + 8, width), jnp.bfloat16),
            jax.ShapeDtypeStruct((2, SUMM, width), jnp.bfloat16),
        ),
        in_specs=[pl.BlockSpec(memory_space=pltpu.SMEM), own, own, own],
        out_specs=(
            pl.BlockSpec((BLK + 8, chunk), lambda c: (0, c)),
            pl.BlockSpec((2, SUMM, chunk), lambda c: (0, 0, c)),
        ),
        compiler_params=pltpu.CompilerParams(vmem_limit_bytes=VMEM),
        name="pack",
    )(frames, keys, values, grad_out)


def dot(left, right, contract):
    return lax.dot_general(
        left, right, (contract, ((), ())), preferred_element_type=jnp.float32
    )


NN = ((1,), (0,))
NT = ((1,), (1,))
TN = ((0,), (0,))


def attend_kernel(
    frames,
    links,
    q_ref,
    k_ref,
    v_ref,
    go_ref,
    up_k_ref,
    down_k_ref,
    cross_k_ref,
    up_v_ref,
    down_v_ref,
    cross_v_ref,
    up_go_ref,
    down_go_ref,
    cross_go_ref,
    summary_ref,
    w_ref,
    dq_ref,
    center_ref,
    to_prev_ref,
    to_next_ref,
    cross_dk_ref,
    cross_dv_ref,
    dsum_ref,
    bias_ref,
):
    device, z_half = place()
    first, frame_count = device * BLK, frames[0]

    @pl.when(pl.program_id(0) == 0)
    def _():
        row = lax.broadcasted_iota(jnp.int32, (BLK, HD), 0)
        seen_left = jnp.where((links[0] == 1) & (device > 0), frame_count - first + BLK, 0)
        seen_right = jnp.where(links[1] == 1, frame_count - first - BLK, 0)
        for part, seen in enumerate((seen_left, frame_count - first, seen_right)):
            bias_ref[pl.ds(part * BLK, BLK), :] = jnp.where(row < seen, 0.0, MASKED)
        row = lax.broadcasted_iota(jnp.int32, (ROWS - WIN, HD), 0)
        source, half, pool = row >> 4, (row >> 3) & 1, row & 7
        block = ((source >> 2) * 2 + (half ^ z_half)) * 4 + (source & 3)
        start = (block * SUMM + pool) * POOL
        bias_ref[WIN:, :] = jnp.where(start < frame_count, 0.0, MASKED)

    x = lax.axis_index("x")
    low, high = x == 0, x == 3

    def one_head(c):

        def window(up_ref, own_ref, down_ref, cross_ref):
            cross = cross_ref[:BLK, c]
            return [
                jnp.where(low, cross, up_ref[:BLK, c]),
                own_ref[:, c],
                jnp.where(high, cross, down_ref[:, c]),
            ]

        keys = jnp.concatenate(
            window(up_k_ref, k_ref, down_k_ref, cross_k_ref) + [summary_ref[:, 0, :, c].reshape(-1, HD)],
            axis=0,
        )
        values = jnp.concatenate(
            window(up_v_ref, v_ref, down_v_ref, cross_v_ref) + [summary_ref[:, 1, :, c].reshape(-1, HD)],
            axis=0,
        )
        queries = q_ref[:, c]

        row = first + lax.broadcasted_iota(jnp.int32, (BLK, 1), 0)
        grad = jnp.where(row < frame_count, go_ref[:, c].astype(jnp.float32), 0.0)
        cross_go = cross_go_ref[:, c].astype(jnp.float32)
        before = jnp.where(low, cross_go, up_go_ref[:, c].astype(jnp.float32))
        after = jnp.where(high, cross_go, down_go_ref[:, c].astype(jnp.float32))
        reach = jnp.concatenate([before[:HALF], grad, after[HALF:]], axis=0)
        shifted = [reach[2 * HALF - j : 2 * HALF - j + BLK] for j in range(KW)]
        total = grad
        for j in range(KW):
            total = total + w_ref[j : j + 1, c] * shifted[j]
        grad_attn = total.astype(jnp.bfloat16)

        scores = dot(keys, queries, NT) * SCALE + bias_ref[...]
        top = jnp.max(scores, axis=0, keepdims=True)
        weight = jnp.exp(scores - top)
        prob = weight * (1.0 / jnp.sum(weight, axis=0, keepdims=True))
        prob_bf = prob.astype(jnp.bfloat16)
        attn = dot(prob_bf, values, TN).astype(jnp.bfloat16).astype(jnp.float32)
        delta = jnp.sum(
            (grad_attn.astype(jnp.float32) * attn).T, axis=0, keepdims=True
        )
        dprob = dot(values, grad_attn, NT)
        dscore = (prob * (dprob - delta)).astype(jnp.bfloat16)

        dq_ref[:, c] = (dot(dscore, keys, TN) * SCALE).astype(jnp.bfloat16)
        for side, part, cross_ref in (
            (0, dot(dscore, queries, NN) * SCALE, cross_dk_ref),
            (1, dot(prob_bf, grad_attn, NN), cross_dv_ref),
        ):
            to_prev_ref[side, :, c] = part[:BLK].astype(jnp.bfloat16)
            center_ref[side, :, c] = part[BLK : 2 * BLK]
            to_next_ref[side, :, c] = part[2 * BLK : WIN].astype(jnp.bfloat16)
            cross_ref[:, c] = jnp.where(high, part[2 * BLK : WIN], part[:BLK]).astype(jnp.bfloat16)
            dsum_ref[:, side, : 2 * SUMM, c] = (
                part[WIN:].astype(jnp.bfloat16).reshape(dsum_ref.shape[0], 2 * SUMM, HD)
            )
        empty = jnp.zeros((SUMM, HD), jnp.float32)
        for j in range(16):
            if j < KW:
                tap = jnp.sum(attn * shifted[j], axis=0, keepdims=True)
                big = tap.astype(jnp.bfloat16).astype(jnp.float32)
                terms = (big + empty, (tap - big) + empty)
            else:
                terms = (empty, empty)
            for side, term in enumerate(terms):
                dsum_ref[j, side, 2 * SUMM :, c] = term.astype(jnp.bfloat16)

    for head in range(HEADS):
        one_head(slice(head * HD, (head + 1) * HD))


def attend(frames, links, queries, keys, values, grad_out, halo_k, halo_v, summary, taps):
    width = queries.shape[1]
    step = HEADS * HD
    smem = pl.BlockSpec(memory_space=pltpu.SMEM)
    own = pl.BlockSpec((BLK, step), lambda h: (0, h))
    pair = pl.BlockSpec((2, BLK, step), lambda h: (0, 0, h))
    many = pl.BlockSpec((16, 2, 2 * SUMM, step), lambda h: (0, 0, 0, h))
    rim = pl.BlockSpec((8, step), lambda h: (BLK // 8, h))
    return pl.pallas_call(
        attend_kernel,
        grid=(width // step,),
        out_shape=(
            jax.ShapeDtypeStruct((BLK, width), jnp.bfloat16),
            jax.ShapeDtypeStruct((2, BLK, width), jnp.float32),
            jax.ShapeDtypeStruct((2, BLK, width), jnp.bfloat16),
            jax.ShapeDtypeStruct((2, BLK, width), jnp.bfloat16),
            jax.ShapeDtypeStruct((BLK, width), jnp.bfloat16),
            jax.ShapeDtypeStruct((BLK, width), jnp.bfloat16),
            jax.ShapeDtypeStruct((16, 2, 3 * SUMM, width), jnp.bfloat16),
        ),
        in_specs=[smem, smem]
        + [own] * 10
        + [rim] * 3
        + [many, pl.BlockSpec((KW, step), lambda h: (0, h))],
        out_specs=(
            own,
            pair,
            pair,
            pair,
            own,
            own,
            pl.BlockSpec((16, 2, 3 * SUMM, step), lambda h: (0, 0, 0, h)),
        ),
        scratch_shapes=[pltpu.VMEM((ROWS, HD), jnp.float32)],
        compiler_params=pltpu.CompilerParams(vmem_limit_bytes=VMEM),
        cost_estimate=pl.CostEstimate(
            flops=6 * 2 * ROWS * BLK * width,
            bytes_accessed=8 * 2**20,
            transcendentals=ROWS * BLK * (width // HD),
        ),
        name="attend",
    )(
        frames, links, queries, keys, values, grad_out, *halo_k, *halo_v, *halo_k, summary, taps
    )


def spread(block, axes, count):
    return lax.all_to_all(
        jnp.broadcast_to(block[None], (count,) + block.shape), axes, 0, 0, tiled=True
    )


def fenced(there, step, *operands):
    shapes = jax.eval_shape(step, *operands)
    return lax.cond(
        there,
        step,
        lambda *_: jax.tree.map(lambda leaf: jnp.zeros(leaf.shape, leaf.dtype), shapes),
        *operands,
    )


def routes():
    rows, width = 8, 4
    up, down, diagonal, outward, inward = [], [], [], [], []
    for row in range(rows):
        at = [row * width + x for x in range(width)]
        up += [(at[x], at[x + 1]) for x in range(width - 1)]
        down += [(at[x + 1], at[x]) for x in range(width - 1)]
        inward += [(at[3], at[2]), (at[0], at[1])]
        outward += [(at[2], at[3]), (at[1], at[0])]
        if row + 1 < rows:
            for ours, theirs in ((at[3], at[3] + 1), (at[2], at[3] + 2)):
                diagonal += [(ours, theirs), (theirs, ours)]
    return up, down, diagonal, outward, inward


def per_device(query_rows, key_rows, value_rows, grad_out, conv_weight, frames, window_links):
    queries, keys, values, grad = query_rows[0], key_rows[0], value_rows[0], grad_out[0]
    up, down, diagonal, outward, inward = routes()
    swap = [(0, 1), (1, 0)]
    x = lax.axis_index("x")
    edge = (x == 0) | (x == 3)
    links = window_links[0, 0]
    there = frames[0] > 0

    up_v = lax.ppermute(values, TM, up)
    down_v = lax.ppermute(values, TM, down)
    packed, own_summary = pack(frames, keys, values, grad)
    other_summary = lax.ppermute(own_summary, "zh", swap)
    up_k = lax.ppermute(packed, TM, up)
    down_k = lax.ppermute(packed, TM, down)
    relay = jnp.pad(jnp.where(x == 1, up_v, down_v), ((0, 8), (0, 0)))
    crossing = jnp.where(edge, packed, relay)
    crossing, other_summary = lax.optimization_barrier((crossing, other_summary))
    cross_k = lax.ppermute(crossing, TM, diagonal)
    summary = fenced(
        there,
        lambda own, other: spread(jnp.concatenate([own, other], axis=1), PLANE, 16),
        own_summary,
        other_summary,
    )
    cross_k, summary = lax.optimization_barrier((cross_k, summary))
    cross_v = lax.ppermute(cross_k[:BLK], TM, outward)

    dq, center, to_prev, to_next, cross_dk, cross_dv, dsum = attend(
        frames,
        links,
        queries,
        keys,
        values,
        grad,
        (up_k, down_k, cross_k),
        (up_v, down_v, cross_v),
        summary,
        conv_weight,
    )

    from_prev = lax.ppermute(to_next, TM, up)
    from_next = lax.ppermute(to_prev, TM, down)
    relay = lax.ppermute(cross_dv, TM, inward)

    relay, dsum = lax.optimization_barrier((relay, dsum))
    dsum = lax.all_to_all(dsum, PLANE, 0, 0, tiled=True)
    dsum = jnp.sum(dsum.astype(jnp.float32), axis=0)
    tap = dsum[0, 2 * SUMM : 2 * SUMM + 1] + dsum[1, 2 * SUMM : 2 * SUMM + 1]
    cross_dk = lax.ppermute(jnp.where(edge, cross_dk, relay), TM, diagonal)

    tap = fenced(there, lambda tap: jnp.sum(spread(tap, LINE, 32), axis=0), tap)
    cross_dk, dsum, tap = lax.optimization_barrier((cross_dk, dsum, tap))
    cross_dv = lax.ppermute(cross_dk, TM, outward)
    taps = fenced(there, lambda tap: spread(tap, PLANE, 16)[:KW, 0], tap)
    other = lax.ppermute(dsum[:, SUMM : 2 * SUMM].astype(jnp.bfloat16), "zh", swap)
    dsum = dsum[:, :SUMM] + other.astype(jnp.float32)

    row = lax.axis_index(TM) * BLK + jnp.arange(BLK, dtype=jnp.int32)
    valid = (row < frames[0]).astype(jnp.float32).reshape(SUMM, POOL)
    share = valid / jnp.maximum(jnp.sum(valid, axis=1, keepdims=True), 1.0)

    def total(side, cross):
        spread_sum = (dsum[side][:, None] * share[:, :, None]).reshape(center[side].shape)
        near = from_prev[side].astype(jnp.float32) + from_next[side].astype(jnp.float32)
        far = jnp.where(edge, cross.astype(jnp.float32), 0.0)
        return (center[side] + near + far + spread_sum).astype(jnp.bfloat16)[None]

    return dq[None], total(0, cross_dk), total(1, cross_dv), taps


def solution(mesh):
    names, sizes = zip(*AXES, strict=True)
    fine = Mesh(mesh.devices.reshape(sizes), names)
    rows = P(DP, TM, None)
    return jax.shard_map(
        per_device,
        mesh=fine,
        in_specs=(rows, rows, rows, rows, P(), P(DP), rows),
        out_specs=(rows, rows, rows, P()),
        check_vma=False,
    )
```

```python
import jax
import jax.numpy as jnp
from jax import lax
from jax.experimental import pallas as pl
from jax.experimental.pallas import tpu as pltpu
from jax.sharding import Mesh
from jax.sharding import PartitionSpec as P

H = 8
HD = 128
HEADS = 4
BLK = 128
POOL = 16
SUMM = BLK // POOL
KW = 9
HALF = 4
WIN = 3 * BLK
ROWS = WIN + 256
SCALE = HD ** (-0.5)
MASKED = -1e30
VMEM = 56 * 2**20
AXES = (("zl", 8), ("core", 2), ("y", 4), ("zh", 2), ("x", 4))
DP = ("zl", "core")
TM = ("y", "zh", "x")
PLANE = ("y", "x")
LINE = ("zl", "core", "zh")


def place():
    z_half = lax.axis_index("zh")
    return (lax.axis_index("y") * 2 + z_half) * 4 + lax.axis_index("x"), z_half


def pack_kernel(frames, k_ref, v_ref, go_ref, packed_ref, summary_ref):
    first, frame_count = place()[0] * BLK, frames[0]
    row = first + lax.broadcasted_iota(jnp.int32, (BLK, 1), 0)
    grad = go_ref[...].astype(jnp.float32)
    grad = jnp.where(row < frame_count, grad, 0.0)
    packed_ref[:BLK, :] = k_ref[...]
    rims = jnp.concatenate([grad[BLK - HALF :], grad[:HALF]], axis=0)
    packed_ref[BLK:, :] = rims.astype(jnp.bfloat16)
    pool = lax.broadcasted_iota(jnp.int32, (SUMM, 1, 1), 0) * POOL + first
    count = jnp.clip(frame_count - pool, 0, POOL)
    frame = pool + lax.broadcasted_iota(jnp.int32, (SUMM, POOL, 1), 1)
    share = jnp.where(
        frame < frame_count, 1.0 / jnp.maximum(count, 1).astype(jnp.float32), 0.0
    )
    for side, ref in ((0, k_ref), (1, v_ref)):
        rows = ref[...].astype(jnp.float32).reshape(SUMM, POOL, ref.shape[1])
        summary_ref[side] = jnp.sum(rows * share, axis=1).astype(jnp.bfloat16)


def pack(frames, keys, values, grad_out):
    width = keys.shape[1]
    chunk = 512
    own = pl.BlockSpec((BLK, chunk), lambda c: (0, c))
    return pl.pallas_call(
        pack_kernel,
        grid=(width // chunk,),
        out_shape=(
            jax.ShapeDtypeStruct((BLK + 8, width), jnp.bfloat16),
            jax.ShapeDtypeStruct((2, SUMM, width), jnp.bfloat16),
        ),
        in_specs=[pl.BlockSpec(memory_space=pltpu.SMEM), own, own, own],
        out_specs=(
            pl.BlockSpec((BLK + 8, chunk), lambda c: (0, c)),
            pl.BlockSpec((2, SUMM, chunk), lambda c: (0, 0, c)),
        ),
        compiler_params=pltpu.CompilerParams(vmem_limit_bytes=VMEM),
        name="pack",
    )(frames, keys, values, grad_out)


def dot(left, right, contract):
    return lax.dot_general(
        left, right, (contract, ((), ())), preferred_element_type=jnp.float32
    )


NN = ((1,), (0,))
NT = ((1,), (1,))
TN = ((0,), (0,))


def attend_kernel(
    frames,
    links,
    q_ref,
    k_ref,
    v_ref,
    go_ref,
    up_k_ref,
    down_k_ref,
    cross_k_ref,
    up_v_ref,
    down_v_ref,
    cross_v_ref,
    up_go_ref,
    down_go_ref,
    cross_go_ref,
    summary_ref,
    w_ref,
    dq_ref,
    center_ref,
    to_prev_ref,
    to_next_ref,
    cross_dk_ref,
    cross_dv_ref,
    dsum_ref,
    bias_ref,
):
    device, z_half = place()
    first, frame_count = device * BLK, frames[0]

    @pl.when(pl.program_id(0) == 0)
    def _():
        row = lax.broadcasted_iota(jnp.int32, (BLK, HD), 0)
        seen_left = jnp.where((links[0] == 1) & (device > 0), frame_count - first + BLK, 0)
        seen_right = jnp.where(links[1] == 1, frame_count - first - BLK, 0)
        for part, seen in enumerate((seen_left, frame_count - first, seen_right)):
            bias_ref[pl.ds(part * BLK, BLK), :] = jnp.where(row < seen, 0.0, MASKED)
        row = lax.broadcasted_iota(jnp.int32, (ROWS - WIN, HD), 0)
        source, half, pool = row >> 4, (row >> 3) & 1, row & 7
        block = ((source >> 2) * 2 + (half ^ z_half)) * 4 + (source & 3)
        start = (block * SUMM + pool) * POOL
        bias_ref[WIN:, :] = jnp.where(start < frame_count, 0.0, MASKED)

    x = lax.axis_index("x")
    low, high = x == 0, x == 3

    def one_head(c):

        def window(up_ref, own_ref, down_ref, cross_ref):
            cross = cross_ref[:BLK, c]
            return [
                jnp.where(low, cross, up_ref[:BLK, c]),
                own_ref[:, c],
                jnp.where(high, cross, down_ref[:, c]),
            ]

        keys = jnp.concatenate(
            window(up_k_ref, k_ref, down_k_ref, cross_k_ref) + [summary_ref[:, 0, :, c].reshape(-1, HD)],
            axis=0,
        )
        values = jnp.concatenate(
            window(up_v_ref, v_ref, down_v_ref, cross_v_ref) + [summary_ref[:, 1, :, c].reshape(-1, HD)],
            axis=0,
        )
        queries = q_ref[:, c]

        row = first + lax.broadcasted_iota(jnp.int32, (BLK, 1), 0)
        grad = jnp.where(row < frame_count, go_ref[:, c].astype(jnp.float32), 0.0)
        cross_go = cross_go_ref[:, c].astype(jnp.float32)
        before = jnp.where(low, cross_go, up_go_ref[:, c].astype(jnp.float32))
        after = jnp.where(high, cross_go, down_go_ref[:, c].astype(jnp.float32))
        reach = jnp.concatenate([before[:HALF], grad, after[HALF:]], axis=0)
        shifted = [reach[2 * HALF - j : 2 * HALF - j + BLK] for j in range(KW)]
        total = grad
        for j in range(KW):
            total = total + w_ref[j : j + 1, c] * shifted[j]
        grad_attn = total.astype(jnp.bfloat16)

        scores = dot(keys, queries, NT) * SCALE + bias_ref[...]
        top = jnp.max(scores, axis=0, keepdims=True)
        weight = jnp.exp(scores - top)
        prob = weight * (1.0 / jnp.sum(weight, axis=0, keepdims=True))
        prob_bf = prob.astype(jnp.bfloat16)
        attn = dot(values, prob_bf, TN).T.astype(jnp.bfloat16).astype(jnp.float32)
        dprob = dot(values, grad_attn, NT)
        delta = jnp.sum(prob * dprob, axis=0, keepdims=True)
        dscore = (prob * (dprob - delta)).astype(jnp.bfloat16)

        dq_ref[:, c] = (dot(keys, dscore, TN).T * SCALE).astype(jnp.bfloat16)
        for side, part, cross_ref in (
            (0, dot(dscore, queries, NN) * SCALE, cross_dk_ref),
            (1, dot(prob_bf, grad_attn, NN), cross_dv_ref),
        ):
            to_prev_ref[side, :, c] = part[:BLK].astype(jnp.bfloat16)
            center_ref[side, :, c] = part[BLK : 2 * BLK]
            to_next_ref[side, :, c] = part[2 * BLK : WIN].astype(jnp.bfloat16)
            cross_ref[:, c] = jnp.where(high, part[2 * BLK : WIN], part[:BLK]).astype(jnp.bfloat16)
            dsum_ref[:, side, : 2 * SUMM, c] = (
                part[WIN:].astype(jnp.bfloat16).reshape(dsum_ref.shape[0], 2 * SUMM, HD)
            )
        empty = jnp.zeros((SUMM, HD), jnp.float32)
        for j in range(16):
            if j < KW:
                tap = jnp.sum(attn * shifted[j], axis=0, keepdims=True)
                big = tap.astype(jnp.bfloat16).astype(jnp.float32)
                terms = (big + empty, (tap - big) + empty)
            else:
                terms = (empty, empty)
            for side, term in enumerate(terms):
                dsum_ref[j, side, 2 * SUMM :, c] = term.astype(jnp.bfloat16)

    for head in range(HEADS):
        one_head(slice(head * HD, (head + 1) * HD))


def attend(frames, links, queries, keys, values, grad_out, halo_k, halo_v, summary, taps):
    width = queries.shape[1]
    step = HEADS * HD
    smem = pl.BlockSpec(memory_space=pltpu.SMEM)
    own = pl.BlockSpec((BLK, step), lambda h: (0, h))
    pair = pl.BlockSpec((2, BLK, step), lambda h: (0, 0, h))
    many = pl.BlockSpec((16, 2, 2 * SUMM, step), lambda h: (0, 0, 0, h))
    rim = pl.BlockSpec((8, step), lambda h: (BLK // 8, h))
    return pl.pallas_call(
        attend_kernel,
        grid=(width // step,),
        out_shape=(
            jax.ShapeDtypeStruct((BLK, width), jnp.bfloat16),
            jax.ShapeDtypeStruct((2, BLK, width), jnp.float32),
            jax.ShapeDtypeStruct((2, BLK, width), jnp.bfloat16),
            jax.ShapeDtypeStruct((2, BLK, width), jnp.bfloat16),
            jax.ShapeDtypeStruct((BLK, width), jnp.bfloat16),
            jax.ShapeDtypeStruct((BLK, width), jnp.bfloat16),
            jax.ShapeDtypeStruct((16, 2, 3 * SUMM, width), jnp.bfloat16),
        ),
        in_specs=[smem, smem]
        + [own] * 10
        + [rim] * 3
        + [many, pl.BlockSpec((KW, step), lambda h: (0, h))],
        out_specs=(
            own,
            pair,
            pair,
            pair,
            own,
            own,
            pl.BlockSpec((16, 2, 3 * SUMM, step), lambda h: (0, 0, 0, h)),
        ),
        scratch_shapes=[pltpu.VMEM((ROWS, HD), jnp.float32)],
        compiler_params=pltpu.CompilerParams(vmem_limit_bytes=VMEM),
        cost_estimate=pl.CostEstimate(
            flops=6 * 2 * ROWS * BLK * width,
            bytes_accessed=8 * 2**20,
            transcendentals=ROWS * BLK * (width // HD),
        ),
        name="attend",
    )(
        frames, links, queries, keys, values, grad_out, *halo_k, *halo_v, *halo_k, summary, taps
    )


def spread(block, axes, count):
    return lax.all_to_all(
        jnp.broadcast_to(block[None], (count,) + block.shape), axes, 0, 0, tiled=True
    )


def fenced(there, step, *operands):
    shapes = jax.eval_shape(step, *operands)
    return lax.cond(
        there,
        step,
        lambda *_: jax.tree.map(lambda leaf: jnp.zeros(leaf.shape, leaf.dtype), shapes),
        *operands,
    )


def routes():
    rows, width = 8, 4
    up, down, diagonal, outward, inward = [], [], [], [], []
    for row in range(rows):
        at = [row * width + x for x in range(width)]
        up += [(at[x], at[x + 1]) for x in range(width - 1)]
        down += [(at[x + 1], at[x]) for x in range(width - 1)]
        inward += [(at[3], at[2]), (at[0], at[1])]
        outward += [(at[2], at[3]), (at[1], at[0])]
        if row + 1 < rows:
            for ours, theirs in ((at[3], at[3] + 1), (at[2], at[3] + 2)):
                diagonal += [(ours, theirs), (theirs, ours)]
    return up, down, diagonal, outward, inward


def per_device(query_rows, key_rows, value_rows, grad_out, conv_weight, frames, window_links):
    queries, keys, values, grad = query_rows[0], key_rows[0], value_rows[0], grad_out[0]
    up, down, diagonal, outward, inward = routes()
    swap = [(0, 1), (1, 0)]
    x = lax.axis_index("x")
    edge = (x == 0) | (x == 3)
    links = window_links[0, 0]
    there = frames[0] > 0

    up_v = lax.ppermute(values, TM, up)
    down_v = lax.ppermute(values, TM, down)
    packed, own_summary = pack(frames, keys, values, grad)
    other_summary = lax.ppermute(own_summary, "zh", swap)
    up_k = lax.ppermute(packed, TM, up)
    down_k = lax.ppermute(packed, TM, down)
    relay = jnp.pad(jnp.where(x == 1, up_v, down_v), ((0, 8), (0, 0)))
    crossing = jnp.where(edge, packed, relay)
    crossing, other_summary = lax.optimization_barrier((crossing, other_summary))
    cross_k = lax.ppermute(crossing, TM, diagonal)
    summary = fenced(
        there,
        lambda own, other: spread(jnp.concatenate([own, other], axis=1), PLANE, 16),
        own_summary,
        other_summary,
    )
    cross_k, summary = lax.optimization_barrier((cross_k, summary))
    cross_v = lax.ppermute(cross_k[:BLK], TM, outward)

    dq, center, to_prev, to_next, cross_dk, cross_dv, dsum = attend(
        frames,
        links,
        queries,
        keys,
        values,
        grad,
        (up_k, down_k, cross_k),
        (up_v, down_v, cross_v),
        summary,
        conv_weight,
    )

    from_prev = lax.ppermute(to_next, TM, up)
    from_next = lax.ppermute(to_prev, TM, down)
    relay = lax.ppermute(cross_dv, TM, inward)

    relay, dsum = lax.optimization_barrier((relay, dsum))
    dsum = lax.all_to_all(dsum, PLANE, 0, 0, tiled=True)
    dsum = jnp.sum(dsum.astype(jnp.float32), axis=0)
    tap = dsum[0, 2 * SUMM : 2 * SUMM + 1] + dsum[1, 2 * SUMM : 2 * SUMM + 1]
    cross_dk = lax.ppermute(jnp.where(edge, cross_dk, relay), TM, diagonal)

    tap = fenced(there, lambda tap: jnp.sum(spread(tap, LINE, 32), axis=0), tap)
    cross_dk, dsum, tap = lax.optimization_barrier((cross_dk, dsum, tap))
    cross_dv = lax.ppermute(cross_dk, TM, outward)
    taps = spread(tap, PLANE, 16)[:KW, 0]
    other = lax.ppermute(dsum[:, SUMM : 2 * SUMM].astype(jnp.bfloat16), "zh", swap)
    dsum = dsum[:, :SUMM] + other.astype(jnp.float32)

    row = lax.axis_index(TM) * BLK + jnp.arange(BLK, dtype=jnp.int32)
    valid = (row < frames[0]).astype(jnp.float32).reshape(SUMM, POOL)
    share = valid / jnp.maximum(jnp.sum(valid, axis=1, keepdims=True), 1.0)

    def total(side, cross):
        spread_sum = (dsum[side][:, None] * share[:, :, None]).reshape(center[side].shape)
        near = from_prev[side].astype(jnp.float32) + from_next[side].astype(jnp.float32)
        far = jnp.where(edge, cross.astype(jnp.float32), 0.0)
        return (center[side] + near + far + spread_sum).astype(jnp.bfloat16)[None]

    return dq[None], total(0, cross_dk), total(1, cross_dv), taps


def solution(mesh):
    names, sizes = zip(*AXES, strict=True)
    fine = Mesh(mesh.devices.reshape(sizes), names)
    rows = P(DP, TM, None)
    return jax.shard_map(
        per_device,
        mesh=fine,
        in_specs=(rows, rows, rows, rows, P(), P(DP), rows),
        out_specs=(rows, rows, rows, P()),
        check_vma=False,
    )
```
